32 devices in a mesh: facet: 8 (over y, x, core), chan: 4 (over z).
Axes of the slice: x: 2, y: 2, z: 4, core: 2. Of those that a mesh axis runs over, the one named last changes fastest.
Arguments:
- visibilities: float32 [8, 4, 4, 2, 256], P('facet', 'chan'), may hold values from -6 to 6
- positions: float32 [8, 4, 4, 2, 256], P('facet', 'chan'), may hold values from 4 to 251
- tracks: int32 [8, 4, 4, 4], P('facet', 'chan'), may hold values from 0 to 1
- counts: int32 [8, 4, 4], P('facet', 'chan'), may hold values from 0 to 4, as said below
- screens: float32 [8, 4, 2, 256, 256], P('facet', 'chan'), may hold values from 0.25 to 4
- offsets: int32 [8, 4, 2, 2], P('facet', 'chan'), may hold values from 0 to 4095, as said below
Outputs:
- image: float32 [2048, 16384], P('facet', 'chan')
The draws below stay inside these ranges and needn't reach their ends.
Inputs may be any that keep to these rules, and one draw needn't show every extreme that they name: Of the 4 block slots from source c to owner d, the first counts[f, d, c] carry data; in every draw some owner receives 4 blocks from every source. Row offsets are below 256 and column offsets below 4096.
All inputs are finite; a program needn't handle non-finite values.
Results may differ from the reference program's by a relative error of at most 0.0003.
Values sent between devices are 32-bit elements; how exact they have to be, the bound alone decides.
No kernel may reach another device: no remote copies, remote signals or barrier semaphores. Data moves between devices by JAX's collectives and lax.ppermute only.
A program may use at most 64 MiB of HBM per device.

```python
import math
import jax
import jax.numpy as jnp
from jax import lax

SUB = 256
TAPS = 8
CH_DEV = 4
CAP = 4
TIMES = 16
SG_DEV = 2
STRIP = 256
BAND = 4096
IMAGE_ROWS = 2048
IMAGE_COLS = 16384
ROWS_OWNER = 1024
N_FACET = 8
N_CHAN = 4


def draw_counts(key, part):
    key = jax.random.fold_in(key, 11)
    first_key, second_key, third_key = jax.random.split(key, 3)
    base_counts = jax.random.randint(first_key, (N_FACET, N_CHAN, N_CHAN), 0, CAP + 1)
    full_facet = jax.random.randint(second_key, (), 0, N_FACET)
    full_owner = jax.random.randint(third_key, (), 0, N_CHAN)
    facet_hit = jnp.arange(N_FACET, dtype=jnp.int32) == full_facet
    owner_hit = jnp.arange(N_CHAN, dtype=jnp.int32) == full_owner
    chosen = facet_hit[:, None, None] & owner_hit[None, :, None]
    return jnp.where(chosen, CAP, base_counts).astype(jnp.int32)


def draw_offsets(key, part):
    key = jax.random.fold_in(key, 23)
    row_key, col_key, late_row_key, late_col_key = jax.random.split(key, 4)
    shape = (N_FACET, N_CHAN, SG_DEV)
    rows = jax.random.randint(row_key, shape, 0, STRIP)
    cols = jax.random.randint(col_key, shape, 0, BAND)
    late_rows = STRIP - 1 - jax.random.randint(late_row_key, shape, 0, SUB // 2)
    late_cols = BAND - 1 - jax.random.randint(late_col_key, shape, 0, SUB // 2)
    first_sub = (jnp.arange(SG_DEV, dtype=jnp.int32) == 0)[None, None, :]
    rows = jnp.where(first_sub, late_rows, rows)
    cols = jnp.where(first_sub, late_cols, cols)
    corner = (jnp.arange(N_FACET * N_CHAN * SG_DEV, dtype=jnp.int32) == 0).reshape(shape)
    rows = jnp.where(corner, STRIP - 1, rows)
    cols = jnp.where(corner, BAND - 1, cols)
    return jnp.stack([rows, cols], axis=-1).astype(jnp.int32)


def place_ends(drawn, key, low, largest):
    spot = [jax.random.randint(jax.random.fold_in(key, axis), (), 0, length) for axis, length in enumerate(drawn.shape)]
    longest = drawn.shape.index(max(drawn.shape))
    neighbour = spot[:longest] + [(spot[longest] + 1) % drawn.shape[longest]] + spot[longest + 1:]
    return drawn.at[tuple(spot)].set(low).at[tuple(neighbour)].set(largest)


def level_of(rng, extent, cuts, low, high):
    loudness, own = 1.0, jax.random.fold_in(rng, 6)
    for position, shards_of in cuts:
        draws = jnp.exp(jax.random.uniform(jax.random.fold_in(own, position), (shards_of,), jnp.float32, low / len(cuts), high / len(cuts)))
        loudness = loudness * jnp.repeat(draws, extent[position] // shards_of).reshape([-1 if axis == position else 1 for axis in range(len(extent))])
    return loudness


def centred(stream_key, extent, deviation, reach, cuts=(), kind=jnp.bfloat16):
    result = jax.random.normal(stream_key, extent, jnp.float32) * deviation
    if len(cuts) > 0:
        result = level_of(stream_key, extent, cuts, -0.22, 0.18) * result
    return jnp.clip(result, min=-reach, max=reach).astype(kind)


def setup_inputs(seed: int = 0) -> dict:
    seeds = jax.random.split(jax.random.key(seed), 7)
    visibilities = centred(seeds[0], (N_FACET, N_CHAN, N_CHAN, 2, CAP * CH_DEV * TIMES), 1.0, 6.0, ((0, 8), (1, 4)), jnp.float32)
    positions = jnp.clip(4.0 + 247.0 * jax.random.uniform(seeds[1], (N_FACET, N_CHAN, N_CHAN, 2, CAP * CH_DEV * TIMES), jnp.float32) ** level_of(seeds[1], (N_FACET, N_CHAN, N_CHAN, 2, CAP * CH_DEV * TIMES), ((0, 8), (1, 4)), -0.2, 0.2), 4.0, 251.0)
    tracks = place_ends(jax.random.randint(seeds[2], (N_FACET, N_CHAN, N_CHAN, CAP), 0, SG_DEV), jax.random.fold_in(seeds[2], 1), 0, SG_DEV - 1).astype(jnp.int32)
    counts = draw_counts(jax.random.fold_in(seeds[6], 71), 0)
    screens = jnp.clip(jnp.exp(math.log(4.0) - 2.7725887 * jax.random.uniform(seeds[4], (N_FACET, N_CHAN, SG_DEV, SUB, SUB), jnp.float32) ** level_of(seeds[4], (N_FACET, N_CHAN, SG_DEV, SUB, SUB), ((0, 8), (1, 4)), -0.2, 0.2)), 0.25, 4.0)
    offsets = draw_offsets(jax.random.fold_in(seeds[6], 71), 0)
    return dict(visibilities=visibilities, positions=positions, tracks=tracks, counts=counts, screens=screens, offsets=offsets)


def taper_weight(offset):
    return jnp.where(jnp.abs(offset) < TAPS / 2, jnp.cos(jnp.pi * offset / TAPS) ** 2, 0.0)

def owner_canvas(pieces):
    own_vis, own_pos, own_tracks, own_counts, own_screens, own_offsets = pieces
    per_block = CH_DEV * TIMES
    block_index = jnp.arange(CAP * per_block, dtype=jnp.int32) // per_block
    live_mask = (block_index[None, :] < own_counts[:, None]).astype(own_vis.dtype)
    target = own_tracks[:, block_index].reshape(-1)
    u_position = own_pos[:, 0].reshape(-1)
    v_position = own_pos[:, 1].reshape(-1)
    real_part = (own_vis[:, 0] * live_mask).reshape(-1)
    imag_part = (own_vis[:, 1] * live_mask).reshape(-1)
    tap_ids = jnp.arange(TAPS, dtype=jnp.int32) - (TAPS // 2 - 1)
    u_cells = jnp.floor(u_position).astype(jnp.int32)[:, None] + tap_ids[None, :]
    v_cells = jnp.floor(v_position).astype(jnp.int32)[:, None] + tap_ids[None, :]
    row_kernel = taper_weight(u_cells.astype(u_position.dtype) - u_position[:, None])
    col_kernel = taper_weight(v_cells.astype(v_position.dtype) - v_position[:, None])
    flat_cells = ((target[:, None, None] * SUB + u_cells[:, :, None]) * SUB + v_cells[:, None, :]).reshape(-1)
    empty_grid = jnp.zeros((SG_DEV * SUB * SUB,), own_vis.dtype)
    real_terms = row_kernel[:, :, None] * (real_part[:, None] * col_kernel)[:, None, :]
    imag_terms = row_kernel[:, :, None] * (imag_part[:, None] * col_kernel)[:, None, :]
    grid_real = empty_grid.at[flat_cells].add(real_terms.reshape(-1)).reshape(SG_DEV, SUB, SUB)
    grid_imag = empty_grid.at[flat_cells].add(imag_terms.reshape(-1)).reshape(SG_DEV, SUB, SUB)
    spectrum = jnp.fft.fft2(lax.complex(grid_real, grid_imag), axes=(1, 2))
    norm_scale = 1.0 / (2.0 * math.sqrt(ROWS_OWNER))
    screened = own_screens * jnp.real(spectrum) * norm_scale
    canvas = jnp.zeros((STRIP + SUB, BAND + SUB), own_vis.dtype)

    def place(index, canvas_now):
        row_start = own_offsets[index, 0].astype(jnp.int32)
        col_start = own_offsets[index, 1].astype(jnp.int32)
        current = lax.dynamic_slice(canvas_now, (row_start, col_start), (SUB, SUB))
        return lax.dynamic_update_slice(canvas_now, current + screened[index], (row_start, col_start))
    return lax.fori_loop(0, SG_DEV, place, canvas)

def facet_strip(visibilities, positions, tracks, counts, screens, offsets, facet_index):
    pieces = (jnp.swapaxes(visibilities[facet_index], 0, 1), jnp.swapaxes(positions[facet_index], 0, 1), tracks[facet_index], counts[facet_index], screens[facet_index], offsets[facet_index])
    canvases = lax.map(owner_canvas, pieces)
    main_part = canvases[:, :, :BAND]
    side_part = canvases[:, :, BAND:]
    main_part = main_part.at[:, :, :SUB].add(jnp.roll(side_part, 1, axis=0))
    return jnp.transpose(main_part, (1, 0, 2)).reshape(STRIP + SUB, N_CHAN * BAND)

def reference(visibilities, positions, tracks, counts, screens, offsets):

    def strip_of(facet_index):
        return facet_strip(visibilities, positions, tracks, counts, screens, offsets, facet_index)
    last_spill = strip_of(jnp.array(N_FACET - 1, dtype=jnp.int32))[STRIP:]

    def accumulate(carry, facet_index):
        whole = strip_of(facet_index)
        rows_out = whole[:STRIP].at[:SUB].add(carry)
        return (whole[STRIP:], rows_out)
    _, strips = lax.scan(accumulate, last_spill, jnp.arange(N_FACET, dtype=jnp.int32))
    return strips.reshape(IMAGE_ROWS, IMAGE_COLS)
```

```python
import functools
import math

import jax
import jax.numpy as jnp
import numpy as np
from jax import lax
from jax.experimental import pallas as pl
from jax.experimental.pallas import tpu as pltpu
from jax.sharding import PartitionSpec as P

TAPS = 8
STRIP = 256
BAND = 4096
SUB = 256
HALF = SUB // 2
BLOCK = 64
TILE = 16
LAST = BAND // SUB - 1


def real_basis():
    x = np.arange(SUB)
    rows = [np.cos(2 * np.pi * ((j * x) % SUB) / SUB) for j in range(HALF + 1)]
    rows += [np.sin(2 * np.pi * ((j * x) % SUB) / SUB) for j in range(1, HALF)]
    table = np.stack(rows).astype(np.float32)
    high = table.astype(jnp.bfloat16)
    low = (table - high.astype(np.float32)).astype(jnp.bfloat16)
    behind = np.concatenate([high, low, high], axis=0)
    ahead = np.concatenate([high.T, high.T, low.T], axis=1)
    return ahead, behind


def halves(value):
    high = value.astype(jnp.bfloat16)
    low = (value - high.astype(jnp.float32)).astype(jnp.bfloat16)
    return high, low


def taper(offset):
    angle = offset * (math.pi / TAPS)
    square = angle * angle
    series = jnp.float32(-1.0 / math.factorial(14))
    for order in range(12, -1, -2):
        sign = 1.0 if order % 4 == 0 else -1.0
        series = series * square + jnp.float32(sign / math.factorial(order))
    return jnp.where(jnp.abs(offset) < TAPS / 2, series * series, 0.0)


def folded(position, rho):
    base = jnp.floor(position) - (TAPS // 2 - 1)

    def cell_at(residue):
        ahead = residue - base
        ahead = ahead - TILE * jnp.floor(ahead * (1.0 / TILE))
        return base + ahead, ahead < TAPS

    cell, inside = cell_at(rho)
    direct = inside & (cell <= HALF)
    near = jnp.where(direct, taper(cell - position), 0.0)
    mirror, inside = cell_at(-rho)
    far = jnp.where(inside & (mirror > HALF), taper(mirror - position), 0.0)
    turn = jnp.where(direct, cell - rho, SUB - mirror - rho) * (1.0 / TILE)
    return near + far, near - far, turn.astype(jnp.bfloat16)


def fill_factors(n, me, tracks, counts, arrived, le, lo, we, wo):
    rows = arrived[0].shape[-1]
    depth = n * rows
    rho = lax.broadcasted_iota(jnp.int32, (TILE, rows), 0).astype(jnp.float32)
    lane_block = lax.broadcasted_iota(jnp.int32, (1, rows), 1) // BLOCK
    zero = jnp.zeros((TILE, rows), jnp.bfloat16)
    for k in range(n):
        source = lax.rem(me - k + n, n)
        live = lane_block < counts[0, 0, source]
        target = jnp.zeros((1, rows), jnp.int32)
        for b in range(rows // BLOCK):
            target = jnp.where(lane_block == b, tracks[0, 0, source, b], target)
        piece = arrived[k][...]
        real = jnp.where(live, piece[0:1], 0.0)
        imag = jnp.where(live, piece[1:2], 0.0)
        u_position = piece[2:3]
        u_even, u_odd, u_turn = folded(u_position, rho)
        v_even, v_odd, v_turn = folded(piece[3:4], rho)
        middle = taper(HALF - u_position)
        places = [(k * rows + part * depth) for part in range(3)]

        def put(ref, row, pair, order):
            for place, which in zip(places, order):
                ref[row : row + TILE, place : place + rows] = pair[which]

        left, right = (0, 1, 0), (0, 0, 1)
        first = target == 0
        evens = [halves(jnp.where(first, u_even, 0.0)), halves(jnp.where(first, 0.0, u_even))]
        odds = [halves(jnp.where(first, u_odd, 0.0)), halves(jnp.where(first, 0.0, u_odd))]
        for turn in range(HALF // TILE):
            chosen = u_turn == turn
            for s in range(2):
                row = s * HALF + turn * TILE
                put(le, row, [jnp.where(chosen, e, zero) for e in evens[s]], left)
                put(lo, row, [jnp.where(chosen, o, zero) for o in odds[s]], left)
        middles = jnp.where(
            (rho == 0) & first, middle, jnp.where((rho == 8) & jnp.logical_not(first), middle, 0.0)
        )
        put(le, 2 * HALF, halves(middles), left)
        for ref, cosine, sine in (
            (we, real * v_even, imag * v_odd),
            (wo, imag * v_even, -real * v_odd),
        ):
            cosine, sine = halves(cosine), halves(sine)
            for turn in range(HALF // TILE):
                chosen = v_turn == turn
                put(ref, turn * TILE, [jnp.where(chosen, c, zero) for c in cosine], right)
                pair = [jnp.where(chosen, c, zero) for c in sine]
                if turn == 0:
                    top = v_turn == HALF // TILE
                    pair = [jnp.where(top, c, p) for c, p in zip(cosine, pair)]
                put(ref, HALF + turn * TILE, pair, right)


def product(a, b, contract):
    return lax.dot_general(a, b, (contract, ((), ())), preferred_element_type=jnp.float32)


def picture_kernel(n, scale, tracks, counts, offsets, *refs):
    arrived = refs[:n]
    screens, ahead, behind, pictures, across, diagonal, le, lo, we, wo = refs[n:]
    me = lax.axis_index("chan")
    fill_factors(n, me, tracks, counts, arrived, le, lo, we, wo)
    even = product(le[...], we[...], ((1,), (1,)))
    odd = product(lo[...], wo[...], ((1,), (1,)))
    row_ids = lax.broadcasted_iota(jnp.int32, (SUB, SUB), 0)
    col_ids = lax.broadcasted_iota(jnp.int32, (SUB, SUB), 1)
    first_row = lax.broadcasted_iota(jnp.int32, (HALF, SUB), 0) == 0
    stays = jnp.zeros((SUB, SUB), jnp.float32)
    falls = jnp.zeros((SUB, SUB), jnp.float32)
    for s in range(2):
        middle = even[2 * HALF + 8 * s : 2 * HALF + 8 * s + 1]
        lower = jnp.where(first_row, middle, odd[s * HALF : (s + 1) * HALF])
        grid = jnp.concatenate([even[s * HALF : (s + 1) * HALF], lower], axis=0)
        high, low = halves(grid)
        half_way = product(
            jnp.concatenate([high, high, low], axis=1), behind[...], ((1,), (0,))
        )
        high, low = halves(half_way)
        image = product(ahead[...], jnp.concatenate([high, low, high], axis=0), ((1,), (0,)))
        image = screens[0, 0, s] * (image * scale)
        row = offsets[0, 0, s, 0]
        col = offsets[0, 0, s, 1]
        shift = lax.rem(col, SUB)
        image = pltpu.roll(pltpu.roll(image, row, 0), shift, 1)
        pictures[s] = image
        beyond = (col_ids < shift) & (col // SUB == LAST)
        stays = stays + jnp.where(beyond & (row_ids >= row), image, 0.0)
        falls = falls + jnp.where(beyond & (row_ids < row), image, 0.0)
    across[...] = stays
    diagonal[...] = falls


def paste_kernel(offsets, offsets_before, own, before, across, diagonal, out):
    out[...] = jnp.zeros_like(out)
    row_ids = lax.broadcasted_iota(jnp.int32, (SUB, SUB), 0)
    col_ids = lax.broadcasted_iota(jnp.int32, (SUB, SUB), 1)
    for pictures, corners, spilled in ((own, offsets, False), (before, offsets_before, True)):
        for s in range(2):
            row = corners[0, 0, s, 0]
            col = corners[0, 0, s, 1]
            shift = lax.rem(col, SUB)
            block = col // SUB
            here = (row_ids < row) if spilled else (row_ids >= row)
            image = jnp.where(here, pictures[s], 0.0)
            place = pl.ds(pl.multiple_of(block * SUB, SUB), SUB)
            out[:, place] += jnp.where(col_ids >= shift, image, 0.0)

            @pl.when(block < LAST)
            def _():
                place = pl.ds(pl.multiple_of((block + 1) * SUB, SUB), SUB)
                out[:, place] += jnp.where(col_ids < shift, image, 0.0)

    out[:, :SUB] += across[...] + diagonal[...]


def shards(mesh, visibilities, positions, tracks, counts, screens, offsets):
    n = mesh.shape["chan"]
    facets = mesh.shape["facet"]
    rows = visibilities.shape[-1]
    me = lax.axis_index("chan")
    vmem = pl.BlockSpec(memory_space=pltpu.VMEM)
    smem = pl.BlockSpec(memory_space=pltpu.SMEM)

    arrived = []
    for k in range(n):
        slot = lax.rem(me + k, n)
        piece = jnp.concatenate(
            [
                lax.dynamic_index_in_dim(visibilities[0, 0], slot, 0, keepdims=False),
                lax.dynamic_index_in_dim(positions[0, 0], slot, 0, keepdims=False),
            ],
            axis=0,
        )
        if k:
            piece = lax.ppermute(piece, "chan", [(i, (i + k) % n) for i in range(n)])
        arrived.append(piece)
    facet_ring = [(i, (i + 1) % facets) for i in range(facets)]
    offsets_before = lax.ppermute(offsets, "facet", facet_ring)

    ahead, behind = real_basis()
    depth = 3 * n * rows
    picture = jax.ShapeDtypeStruct((SUB, SUB), jnp.float32)
    pictures, across, diagonal = pl.pallas_call(
        functools.partial(picture_kernel, n, 1.0 / (2.0 * math.sqrt(n * rows))),
        out_shape=(jax.ShapeDtypeStruct((2, SUB, SUB), jnp.float32), picture, picture),
        in_specs=[smem] * 3 + [vmem] * (n + 3),
        out_specs=(vmem, vmem, vmem),
        scratch_shapes=[
            pltpu.VMEM((2 * HALF + TILE, depth), jnp.bfloat16),
            pltpu.VMEM((2 * HALF, depth), jnp.bfloat16),
            pltpu.VMEM((SUB, depth), jnp.bfloat16),
            pltpu.VMEM((SUB, depth), jnp.bfloat16),
        ],
        compiler_params=pltpu.CompilerParams(vmem_limit_bytes=56 * 1024 * 1024),
    )(tracks, counts, offsets, *arrived, screens, jnp.asarray(ahead), jnp.asarray(behind))

    before = lax.ppermute(pictures, "facet", facet_ring)
    across = lax.ppermute(across, "chan", [(i, (i + 1) % n) for i in range(n)])
    diagonal = lax.ppermute(
        diagonal,
        ("facet", "chan"),
        [
            (f * n + d, (f + 1) % facets * n + (d + 1) % n)
            for f in range(facets)
            for d in range(n)
        ],
    )
    return pl.pallas_call(
        paste_kernel,
        out_shape=jax.ShapeDtypeStruct((STRIP, BAND), jnp.float32),
        in_specs=[smem] * 2 + [vmem] * 4,
        out_specs=vmem,
        compiler_params=pltpu.CompilerParams(vmem_limit_bytes=56 * 1024 * 1024),
    )(offsets, offsets_before, pictures, before, across, diagonal)


def solution(mesh):
    return jax.shard_map(
        functools.partial(shards, mesh),
        mesh=mesh,
        in_specs=(
            P("facet", "chan", None, None, None),
            P("facet", "chan", None, None, None),
            P("facet", "chan", None, None),
            P("facet", "chan", None),
            P("facet", "chan", None, None, None),
            P("facet", "chan", None, None),
        ),
        out_specs=P("facet", "chan"),
        check_vma=False,
    )
```

```python
import functools
import math

import jax
import jax.numpy as jnp
from jax import lax
from jax.experimental import pallas as pl
from jax.experimental.pallas import tpu as pltpu
from jax.sharding import PartitionSpec as P

TAPS = 8
STRIP = 256
BAND = 4096
SUB = 256
HALF = SUB // 2
BLOCK = 64
TILE = 16
LAST = BAND // SUB - 1


def tables_kernel(ahead, behind):
    shape = (SUB, SUB)
    for across, out in ((1, ahead), (0, behind)):
        j = lax.broadcasted_iota(jnp.int32, shape, across)
        x = lax.broadcasted_iota(jnp.int32, shape, 1 - across)
        turn = jnp.where(j > HALF, (j - HALF) * x + 3 * SUB // 4, j * x) & (SUB - 1)
        turn = jnp.minimum(turn, SUB - turn).astype(jnp.float32)
        half_angle = cosine(turn * (math.pi / SUB))
        high, low = halves(2.0 * half_angle * half_angle - 1.0)
        parts = (high, high, low) if across else (high, low, high)
        out[...] = jnp.concatenate(parts, axis=across)


def halves(value):
    high = value.astype(jnp.bfloat16)
    low = (value - high.astype(jnp.float32)).astype(jnp.bfloat16)
    return high, low


def cosine(angle):
    square = angle * angle
    series = jnp.float32(-1.0 / math.factorial(14))
    for order in range(12, -1, -2):
        sign = 1.0 if order % 4 == 0 else -1.0
        series = series * square + jnp.float32(sign / math.factorial(order))
    return series


def taper(offset):
    series = cosine(offset * (math.pi / TAPS))
    return jnp.where(jnp.abs(offset) < TAPS / 2, series * series, 0.0)


def folded(position, rho):
    base = jnp.floor(position) - (TAPS // 2 - 1)

    def cell_at(residue):
        ahead = residue - base
        ahead = ahead - TILE * jnp.floor(ahead * (1.0 / TILE))
        return base + ahead, ahead < TAPS

    cell, inside = cell_at(rho)
    direct = inside & (cell <= HALF)
    near = jnp.where(direct, taper(cell - position), 0.0)
    mirror, inside = cell_at(-rho)
    far = jnp.where(inside & (mirror > HALF), taper(mirror - position), 0.0)
    turn = jnp.where(direct, cell - rho, SUB - mirror - rho) * (1.0 / TILE)
    return near + far, near - far, turn.astype(jnp.bfloat16)


def pack_kernel(n, tracks, counts, offsets, visibilities, positions, *outs):
    me = lax.axis_index("chan")
    base = outs[n - 1]
    base[...] = jnp.zeros_like(base)
    for k in range(n):
        slot = lax.rem(me + k, n)
        out = outs[k - 1] if k else base.at[0]
        out[0:2] = visibilities[0, 0, slot]
        out[2:4] = positions[0, 0, slot]
    capacity = tracks.shape[-1]
    values = [tracks[0, 0, c, b] for c in range(n) for b in range(capacity)]
    values += [counts[0, 0, c] for c in range(n)]
    values += [offsets[0, 0, s, axis] for s in range(2) for axis in range(2)]
    lane = lax.broadcasted_iota(jnp.int32, base.shape[1:], 1)
    numbers = jnp.zeros(lane.shape, jnp.int32)
    for place, value in enumerate(values):
        numbers = jnp.where(lane == place, value, numbers)
    base[1] = numbers.astype(jnp.float32)


def fill_factors(n, me, numbers, pieces, le, lo, we, wo):
    rows = pieces.shape[-1]
    depth = n * rows
    capacity = rows // BLOCK
    rho = lax.broadcasted_iota(jnp.int32, (TILE, rows), 0).astype(jnp.float32)
    lane_block = lax.broadcasted_iota(jnp.int32, (1, rows), 1) // BLOCK
    zero = jnp.zeros((TILE, rows), jnp.bfloat16)
    for k in range(n):
        source = lax.rem(me - k + n, n)
        live = lane_block.astype(jnp.float32) < numbers[0, n * capacity + source]
        target = jnp.zeros((1, rows), jnp.float32)
        for b in range(capacity):
            target = jnp.where(lane_block == b, numbers[0, source * capacity + b], target)
        piece = pieces[k + 1 if k else 0]
        real = jnp.where(live, piece[0:1], 0.0)
        imag = jnp.where(live, piece[1:2], 0.0)
        u_position = piece[2:3]
        u_even, u_odd, u_turn = folded(u_position, rho)
        v_even, v_odd, v_turn = folded(piece[3:4], rho)
        middle = taper(HALF - u_position)
        places = [(k * rows + part * depth) for part in range(3)]

        def put(ref, row, pair, order):
            for place, which in zip(places, order):
                ref[row : row + TILE, place : place + rows] = pair[which]

        left, right = (0, 1, 0), (0, 0, 1)
        first = target == 0.0
        evens = [halves(jnp.where(first, u_even, 0.0)), halves(jnp.where(first, 0.0, u_even))]
        odds = [halves(jnp.where(first, u_odd, 0.0)), halves(jnp.where(first, 0.0, u_odd))]
        for turn in range(HALF // TILE):
            chosen = u_turn == turn
            for s in range(2):
                row = s * HALF + turn * TILE
                put(le, row, [jnp.where(chosen, e, zero) for e in evens[s]], left)
                put(lo, row, [jnp.where(chosen, o, zero) for o in odds[s]], left)
        middles = jnp.where(
            (rho == 0) & first, middle, jnp.where((rho == 8) & jnp.logical_not(first), middle, 0.0)
        )
        put(le, 2 * HALF, halves(middles), left)
        for ref, cosine, sine in (
            (we, real * v_even, imag * v_odd),
            (wo, imag * v_even, -real * v_odd),
        ):
            cosine, sine = halves(cosine), halves(sine)
            for turn in range(HALF // TILE):
                chosen = v_turn == turn
                put(ref, turn * TILE, [jnp.where(chosen, c, zero) for c in cosine], right)
                pair = [jnp.where(chosen, c, zero) for c in sine]
                if turn == 0:
                    top = v_turn == HALF // TILE
                    pair = [jnp.where(top, c, p) for c, p in zip(cosine, pair)]
                put(ref, HALF + turn * TILE, pair, right)


def product(a, b, contract):
    return lax.dot_general(a, b, (contract, ((), ())), preferred_element_type=jnp.float32)


def picture_kernel(n, scale, spilled, *refs):
    count = 5 if spilled else 4
    payload_in, screens_in, ahead_in, behind_in = refs[:4]
    pictures, across = refs[count : count + 2]
    pieces, numbers, screens, ahead, behind, le, lo, we, wo, sems = refs[count + 2 :]
    copies = [
        pltpu.make_async_copy(source, target, sems.at[i])
        for i, (source, target) in enumerate(
            (
                (payload_in.at[1, pl.ds(0, 1)], numbers),
                (payload_in, pieces),
                (behind_in, behind),
                (ahead_in, ahead),
                (screens_in.at[0, 0], screens),
            )
        )
    ]
    for copy in copies:
        copy.start()
    copies[0].wait()
    copies[1].wait()
    me = lax.axis_index("chan")
    fill_factors(n, me, numbers, pieces, le, lo, we, wo)
    even = product(le[...], we[...], ((1,), (1,)))
    odd = product(lo[...], wo[...], ((1,), (1,)))
    copies[2].wait()
    copies[3].wait()
    copies[4].wait()
    row_ids = lax.broadcasted_iota(jnp.int32, (SUB, SUB), 0)
    col_ids = lax.broadcasted_iota(jnp.int32, (SUB, SUB), 1)
    first_row = lax.broadcasted_iota(jnp.int32, (HALF, SUB), 0) == 0
    total = refs[4][...] if spilled else jnp.zeros((SUB, SUB), jnp.float32)
    corner = n * (pieces.shape[-1] // BLOCK + 1)
    for s in range(2):
        middle = even[2 * HALF + 8 * s : 2 * HALF + 8 * s + 1]
        lower = jnp.where(first_row, middle, odd[s * HALF : (s + 1) * HALF])
        grid = jnp.concatenate([even[s * HALF : (s + 1) * HALF], lower], axis=0)
        high, low = halves(grid)
        half_way = product(
            jnp.concatenate([high, high, low], axis=1), behind[...], ((1,), (0,))
        )
        high, low = halves(half_way)
        image = product(ahead[...], jnp.concatenate([high, low, high], axis=0), ((1,), (0,)))
        image = screens[s] * (image * scale)
        row = numbers[0, corner + 2 * s].astype(jnp.int32)
        col = numbers[0, corner + 2 * s + 1].astype(jnp.int32)
        shift = lax.rem(col, SUB)
        image = pltpu.roll(pltpu.roll(image, row, 0), shift, 1)
        here = (row_ids < row) if spilled else (row_ids >= row)
        image = jnp.where(here, image, 0.0)
        pictures[s] = image
        beyond = (col_ids < shift) & (col // SUB == LAST)
        total = total + jnp.where(beyond, image, 0.0)
    across[...] = total


def paste_kernel(n, corner, payload_in, payload_before, own, before, out, numbers, sems):
    copies = [
        pltpu.make_async_copy(source.at[1, pl.ds(0, 1)], numbers.at[pl.ds(i, 1)], sems.at[i])
        for i, source in enumerate((payload_in, payload_before))
    ]
    for copy in copies:
        copy.start()
    out[...] = jnp.zeros_like(out)
    for copy in copies:
        copy.wait()
    col_ids = lax.broadcasted_iota(jnp.int32, (SUB, SUB), 1)
    for i, pictures in enumerate((own, before)):
        for s in range(2):
            col = numbers[i, corner + 2 * s + 1].astype(jnp.int32)
            shift = lax.rem(col, SUB)
            block = col // SUB
            image = pictures[s]
            place = pl.ds(pl.multiple_of(block * SUB, SUB), SUB)
            out[:, place] += jnp.where(col_ids >= shift, image, 0.0)

            @pl.when(block < LAST)
            def _():
                place = pl.ds(pl.multiple_of((block + 1) * SUB, SUB), SUB)
                out[:, place] += jnp.where(col_ids < shift, image, 0.0)


def finish_kernel(image_in, across_in, image_out, block, across, sems):
    window = pl.ds(0, SUB)
    copies = [
        pltpu.make_async_copy(image_in.at[:, window], block, sems.at[0]),
        pltpu.make_async_copy(across_in, across, sems.at[1]),
    ]
    for copy in copies:
        copy.start()
    for copy in copies:
        copy.wait()
    block[...] += across[...]
    copy = pltpu.make_async_copy(block, image_out.at[:, window], sems.at[2])
    copy.start()
    copy.wait()


def shards(mesh, visibilities, positions, tracks, counts, screens, offsets):
    n = mesh.shape["chan"]
    facets = mesh.shape["facet"]
    rows = visibilities.shape[-1]
    vmem = pl.BlockSpec(memory_space=pltpu.VMEM)
    anywhere = pl.BlockSpec(memory_space=pl.ANY)
    hbm = pl.BlockSpec(memory_space=pltpu.HBM)
    facet_ring = [(i, (i + 1) % facets) for i in range(facets)]

    packed = pl.pallas_call(
        functools.partial(pack_kernel, n),
        out_shape=(jax.ShapeDtypeStruct((4, rows), jnp.float32),) * (n - 1)
        + (jax.ShapeDtypeStruct((2, 4, rows), jnp.float32),),
        in_specs=[pl.BlockSpec(memory_space=pltpu.SMEM)] * 3 + [vmem] * 2,
        out_specs=(vmem,) * n,
        compiler_params=pltpu.CompilerParams(vmem_limit_bytes=56 << 20),
    )(tracks, counts, offsets, visibilities, positions)
    arrived = [
        lax.ppermute(packed[k - 1], "chan", [(i, (i + k) % n) for i in range(n)])
        for k in range(1, n)
    ]
    screens_before = lax.ppermute(screens, "facet", facet_ring)
    base, screens_before = lax.optimization_barrier((packed[n - 1], screens_before))
    payload = jnp.concatenate([base] + [piece[None] for piece in arrived], axis=0)
    payload = jnp.pad(payload, ((0, 0), (0, 4), (0, 0)))
    payload_before = lax.ppermute(payload, "facet", facet_ring)

    ahead, behind = pl.pallas_call(
        tables_kernel,
        out_shape=(
            jax.ShapeDtypeStruct((SUB, 3 * SUB), jnp.bfloat16),
            jax.ShapeDtypeStruct((3 * SUB, SUB), jnp.bfloat16),
        ),
        out_specs=(vmem, vmem),
        compiler_params=pltpu.CompilerParams(vmem_limit_bytes=8 << 20),
        cost_estimate=pl.CostEstimate(flops=4 << 20, bytes_accessed=1 << 20, transcendentals=0),
    )()
    depth = 3 * n * rows
    picture = jax.ShapeDtypeStruct((SUB, SUB), jnp.float32)
    scale = 1.0 / (2.0 * math.sqrt(n * rows))
    factor_rows = 4 * HALF + TILE + 2 * SUB
    room = 24 + (2 * factor_rows * depth >> 20)

    def pictures_of(spilled, *operands):
        return pl.pallas_call(
            functools.partial(picture_kernel, n, scale, spilled),
            out_shape=(jax.ShapeDtypeStruct((2, SUB, SUB), jnp.float32), picture),
            in_specs=[anywhere] * 4
            + [vmem] * (len(operands) - 4),
            out_specs=(vmem, vmem),
            scratch_shapes=[
                pltpu.VMEM((n + 1, 8, rows), jnp.float32),
                pltpu.SMEM((1, rows), jnp.float32),
                pltpu.VMEM((2, SUB, SUB), jnp.float32),
                pltpu.VMEM(ahead.shape, jnp.bfloat16),
                pltpu.VMEM(behind.shape, jnp.bfloat16),
                pltpu.VMEM((2 * HALF + TILE, depth), jnp.bfloat16),
                pltpu.VMEM((2 * HALF, depth), jnp.bfloat16),
                pltpu.VMEM((SUB, depth), jnp.bfloat16),
                pltpu.VMEM((SUB, depth), jnp.bfloat16),
                pltpu.SemaphoreType.DMA((5,)),
            ],
            compiler_params=pltpu.CompilerParams(vmem_limit_bytes=max(room, 0 if spilled else 52) << 20),
            cost_estimate=pl.CostEstimate(
                flops=2 * depth * SUB * SUB * 4, bytes_accessed=4 << 20, transcendentals=0
            ),
        )(*operands)

    own, across = pictures_of(False, payload, screens, ahead, behind)
    before, across = pictures_of(True, payload_before, screens_before, ahead, behind, across)
    across = lax.ppermute(across, "chan", [(i, (i + 1) % n) for i in range(n)])
    image = pl.pallas_call(
        functools.partial(paste_kernel, n, n * (rows // BLOCK + 1)),
        out_shape=jax.ShapeDtypeStruct((STRIP, BAND), jnp.float32),
        in_specs=[anywhere] * 2 + [vmem] * 2,
        out_specs=vmem,
        scratch_shapes=[pltpu.SMEM((2, rows), jnp.float32), pltpu.SemaphoreType.DMA((2,))],
        compiler_params=pltpu.CompilerParams(vmem_limit_bytes=16 << 20),
        cost_estimate=pl.CostEstimate(flops=1 << 20, bytes_accessed=12 << 20, transcendentals=0),
    )(payload, payload_before, own, before)
    return pl.pallas_call(
        finish_kernel,
        out_shape=jax.ShapeDtypeStruct((STRIP, BAND), jnp.float32),
        in_specs=[anywhere] * 2,
        out_specs=anywhere,
        scratch_shapes=[
            pltpu.VMEM((STRIP, SUB), jnp.float32),
            pltpu.VMEM((STRIP, SUB), jnp.float32),
            pltpu.SemaphoreType.DMA((3,)),
        ],
        input_output_aliases={0: 0},
        compiler_params=pltpu.CompilerParams(vmem_limit_bytes=4 << 20),
    )(image, across)


def solution(mesh):
    return jax.shard_map(
        functools.partial(shards, mesh),
        mesh=mesh,
        in_specs=(
            P("facet", "chan", None, None, None),
            P("facet", "chan", None, None, None),
            P("facet", "chan", None, None),
            P("facet", "chan", None),
            P("facet", "chan", None, None, None),
            P("facet", "chan", None, None),
        ),
        out_specs=P("facet", "chan"),
        check_vma=False,
    )
```

```python
import functools
import math

import jax
import jax.numpy as jnp
from jax import lax
from jax.experimental import pallas as pl
from jax.experimental.pallas import tpu as pltpu
from jax.sharding import PartitionSpec as P

TAPS = 8
STRIP = 256
BAND = 4096
SUB = 256
HALF = SUB // 2
BLOCK = 64
TILE = 16
LAST = BAND // SUB - 1
PARTS = 8


def numbers_kernel(n, tracks, counts, offsets, out):
    me = lax.axis_index("chan")
    lane = lax.broadcasted_iota(jnp.int32, (1, out.shape[1]), 1)
    block = lane // BLOCK
    lines = []
    for k in range(n):
        source = sender(n, me, k)
        target = jnp.zeros_like(lane)
        for b in range(tracks.shape[-1]):
            target = jnp.where(block == b, tracks[0, 0, source, b], target)
        lines += [target, jnp.where(block < counts[0, 0, source], 1, 0)]
    corners = jnp.zeros_like(lane)
    for place in range(4):
        corners = jnp.where(lane == place, offsets[0, 0, place // 2, place % 2], corners)
    lines += [corners] * (out.shape[0] - 2 * n)
    out[...] = jnp.concatenate(lines, axis=0).astype(jnp.float32)


def tables_kernel(numbers_in, ahead, behind, numbers):
    numbers[...] = numbers_in[...]
    shape = (SUB, SUB)
    for across, out in ((1, ahead), (0, behind)):
        j = lax.broadcasted_iota(jnp.int32, shape, across)
        x = lax.broadcasted_iota(jnp.int32, shape, 1 - across)
        turn = jnp.where(j > HALF, (j - HALF) * x + 3 * SUB // 4, j * x) & (SUB - 1)
        turn = jnp.minimum(turn, SUB - turn).astype(jnp.float32)
        half_angle = cosine(turn * (math.pi / SUB))
        high, low = halves(2.0 * half_angle * half_angle - 1.0)
        out[:SUB] = high
        out[SUB:] = low


def halves(value):
    high = value.astype(jnp.bfloat16)
    low = (value - high.astype(jnp.float32)).astype(jnp.bfloat16)
    return high, low


def cosine(angle):
    square = angle * angle
    series = jnp.float32(-1.0 / math.factorial(14))
    for order in range(12, -1, -2):
        sign = 1.0 if order % 4 == 0 else -1.0
        series = series * square + jnp.float32(sign / math.factorial(order))
    return series


def taper(offset):
    series = cosine(offset * (math.pi / TAPS))
    return jnp.where(jnp.abs(offset) < TAPS / 2, series * series, 0.0)


def folded(position, rho):
    base = jnp.floor(position) - (TAPS // 2 - 1)

    def cell_at(residue):
        ahead = residue - base
        ahead = ahead - TILE * jnp.floor(ahead * (1.0 / TILE))
        return base + ahead, ahead < TAPS

    cell, inside = cell_at(rho)
    direct = inside & (cell <= HALF)
    near = jnp.where(direct, taper(cell - position), 0.0)
    mirror, inside = cell_at(-rho)
    far = jnp.where(inside & (mirror > HALF), taper(mirror - position), 0.0)
    turn = jnp.where(direct, cell - rho, SUB - mirror - rho) * (1.0 / TILE)
    return near + far, near - far, turn.astype(jnp.bfloat16)


def sender(n, me, k):
    return me ^ k if n == 4 else lax.rem(me - k + n, n)


def exchange(n, me, visibilities, positions, numbers):
    def slot(index):
        parts = [lax.dynamic_index_in_dim(a[0, 0], index, 0, False) for a in (visibilities, positions)]
        return jnp.concatenate(parts, axis=0)

    def swap(piece, bit):
        return lax.ppermute(piece, "chan", [(i, i ^ bit) for i in range(n)])

    if n != 4:
        pieces = [slot(me)]
        for k in range(1, n):
            ring = [(i, (i + k) % n) for i in range(n)]
            pieces.append(lax.ppermute(slot(lax.rem(me + k, n)), "chan", ring))
        return pieces
    near = swap(jnp.concatenate([slot(me ^ 1), slot(me ^ 3)], axis=0), 1)
    near, numbers = lax.optimization_barrier((near, numbers))
    far = swap(jnp.concatenate([slot(me ^ 2), near[4:]], axis=0), 2)
    return [slot(me), near[:4], far]


def fill_factors(n, payload, le, lo, we, wo):
    rows = payload.shape[-1]
    rho = lax.broadcasted_iota(jnp.int32, (TILE, rows), 0).astype(jnp.float32)
    zero = jnp.zeros((TILE, rows), jnp.bfloat16)
    for k in range(n):
        piece = payload[4 * k : 4 * k + 4]
        target = payload[4 * n + 2 * k : 4 * n + 2 * k + 1]
        live = payload[4 * n + 2 * k + 1 : 4 * n + 2 * k + 2]
        real = piece[0:1] * live
        imag = piece[1:2] * live
        u_position = piece[2:3]
        u_even, u_odd, u_turn = folded(u_position, rho)
        v_even, v_odd, v_turn = folded(piece[3:4], rho)
        middle = taper(HALF - u_position)
        place = pl.ds(k * rows, rows)

        def put(ref, row, pair):
            for part, value in enumerate(pair):
                start = part * (ref.shape[0] // 2) + row
                ref[start : start + TILE, place] = value

        first = target == 0.0
        evens = [halves(jnp.where(first, u_even, 0.0)), halves(jnp.where(first, 0.0, u_even))]
        odds = [halves(jnp.where(first, u_odd, 0.0)), halves(jnp.where(first, 0.0, u_odd))]
        for turn in range(HALF // TILE):
            chosen = u_turn == turn
            for s in range(2):
                row = s * HALF + turn * TILE
                put(le, row, [jnp.where(chosen, e, zero) for e in evens[s]])
                put(lo, row, [jnp.where(chosen, o, zero) for o in odds[s]])
        middles = jnp.where(
            (rho == 0) & first, middle, jnp.where((rho == 8) & jnp.logical_not(first), middle, 0.0)
        )
        put(le, 2 * HALF, halves(middles))
        for ref, cosine, sine in (
            (we, real * v_even, imag * v_odd),
            (wo, imag * v_even, -real * v_odd),
        ):
            cosine, sine = halves(cosine), halves(sine)
            for turn in range(HALF // TILE):
                chosen = v_turn == turn
                put(ref, turn * TILE, [jnp.where(chosen, c, zero) for c in cosine])
                pair = [jnp.where(chosen, c, zero) for c in sine]
                if turn == 0:
                    top = v_turn == HALF // TILE
                    pair = [jnp.where(top, c, p) for c, p in zip(cosine, pair)]
                put(ref, HALF + turn * TILE, pair)


def product(a, b, contract):
    rows, half = a.shape[0] // 2, b.shape[0] // 2

    def dot(left, right):
        numbers = (((1,), (contract,)), ((), ()))
        return lax.dot_general(left, right, numbers, preferred_element_type=jnp.float32)

    main = dot(a, b[:half])
    return main[:rows] + main[rows:] + dot(a[:rows], b[half:])


def picture_kernel(n, scale, spilled, *refs):
    count = 5 if spilled else 4
    payload, screens_in, ahead, behind = refs[:4]
    pictures, across = refs[count : count + 2]
    corners, le, lo, we, wo, sems = refs[count + 2 : count + 8]
    copies = [pltpu.make_async_copy(payload.at[pl.ds(6 * n, 1)], corners, sems.at[0])]
    if spilled:
        screens = screens_in.at[0, 0]
    else:
        screens = refs[-1]
        for part in range(PARTS):
            place = (part * 2 // PARTS, pl.ds(part % (PARTS // 2) * (2 * SUB // PARTS), 2 * SUB // PARTS))
            copies.append(
                pltpu.make_async_copy(
                    screens_in.at[0, 0].at[place], screens.at[place], sems.at[1 + part]
                )
            )
    for copy in copies:
        copy.start()
    fill_factors(n, payload, le, lo, we, wo)
    even = product(le[...], we[...], 1)
    odd = product(lo[...], wo[...], 1)
    row_ids = lax.broadcasted_iota(jnp.int32, (SUB, SUB), 0)
    col_ids = lax.broadcasted_iota(jnp.int32, (SUB, SUB), 1)
    first_row = lax.broadcasted_iota(jnp.int32, (HALF, SUB), 0) == 0
    total = refs[4][...] if spilled else jnp.zeros((SUB, SUB), jnp.float32)
    grids = []
    for s in range(2):
        middle = even[2 * HALF + 8 * s : 2 * HALF + 8 * s + 1]
        lower = jnp.where(first_row, middle, odd[s * HALF : (s + 1) * HALF])
        grids += [even[s * HALF : (s + 1) * HALF], lower]
    half_way = product(
        jnp.concatenate(halves(jnp.concatenate(grids, axis=0)), axis=0), behind[...], 0
    )
    for s in range(2):
        image = jnp.concatenate(halves(half_way[s * SUB : (s + 1) * SUB]), axis=0)
        image = product(ahead[...], image, 0)
        if s == 0:
            copies[0].wait()
        for copy in copies[1 + s * PARTS // 2 : 1 + (s + 1) * PARTS // 2]:
            copy.wait()
        image = screens[s] * (image * scale)
        row = corners[0, 2 * s].astype(jnp.int32)
        col = corners[0, 2 * s + 1].astype(jnp.int32)
        shift = lax.rem(col, SUB)
        image = pltpu.roll(pltpu.roll(image, row, 0), shift, 1)
        here = (row_ids < row) if spilled else (row_ids >= row)
        image = jnp.where(here, image, 0.0)
        pictures[s] = image
        beyond = (col_ids < shift) & (col // SUB == LAST)
        total = total + jnp.where(beyond, image, 0.0)
    across[...] = total


def paste_kernel(n, payload_in, payload_before, own, before, out, block_out, corners, sems):
    copies = [
        pltpu.make_async_copy(source.at[pl.ds(6 * n, 1)], corners.at[pl.ds(i, 1)], sems.at[i])
        for i, source in enumerate((payload_in, payload_before))
    ]
    for copy in copies:
        copy.start()
    out[...] = jnp.zeros_like(out)
    for copy in copies:
        copy.wait()
    col_ids = lax.broadcasted_iota(jnp.int32, (SUB, SUB), 1)
    for i, pictures in enumerate((own, before)):
        for s in range(2):
            col = corners[i, 2 * s + 1].astype(jnp.int32)
            shift = lax.rem(col, SUB)
            block = col // SUB
            image = pictures[s]
            place = pl.ds(pl.multiple_of(block * SUB, SUB), SUB)
            out[:, place] += jnp.where(col_ids >= shift, image, 0.0)

            @pl.when(block < LAST)
            def _():
                place = pl.ds(pl.multiple_of((block + 1) * SUB, SUB), SUB)
                out[:, place] += jnp.where(col_ids < shift, image, 0.0)

    block_out[...] = out[:, :SUB]


def finish_kernel(image_in, block, across, image_out, total, sem):
    total[...] = block[...] + across[...]
    copy = pltpu.make_async_copy(total, image_out.at[:, pl.ds(0, SUB)], sem)
    copy.start()
    copy.wait()


def shards(mesh, visibilities, positions, tracks, counts, screens, offsets):
    n = mesh.shape["chan"]
    facets = mesh.shape["facet"]
    rows = visibilities.shape[-1]
    vmem = pl.BlockSpec(memory_space=pltpu.VMEM)
    anywhere = pl.BlockSpec(memory_space=pl.ANY)
    hbm = pl.BlockSpec(memory_space=pltpu.HBM)
    facet_ring = [(i, (i + 1) % facets) for i in range(facets)]

    numbers = pl.pallas_call(
        functools.partial(numbers_kernel, n),
        out_shape=jax.ShapeDtypeStruct((2 * n + 8, rows), jnp.float32),
        in_specs=[pl.BlockSpec(memory_space=pltpu.SMEM)] * 3,
        out_specs=vmem,
        compiler_params=pltpu.CompilerParams(vmem_limit_bytes=56 << 20),
    )(tracks, counts, offsets)
    pieces = exchange(n, lax.axis_index("chan"), visibilities, positions, numbers)
    screens_before = lax.ppermute(screens, "facet", facet_ring)
    ahead, behind, numbers = pl.pallas_call(
        tables_kernel,
        out_shape=(
            jax.ShapeDtypeStruct((2 * SUB, SUB), jnp.bfloat16),
            jax.ShapeDtypeStruct((2 * SUB, SUB), jnp.bfloat16),
            jax.ShapeDtypeStruct((2 * n + 8, rows), jnp.float32),
        ),
        in_specs=[vmem],
        out_specs=(vmem, vmem, vmem),
        compiler_params=pltpu.CompilerParams(vmem_limit_bytes=8 << 20),
        cost_estimate=pl.CostEstimate(flops=4 << 20, bytes_accessed=1 << 20, transcendentals=0),
    )(numbers)
    pieces[0], screens_before = lax.optimization_barrier((pieces[0], screens_before))
    payload = jnp.concatenate(pieces + [numbers], axis=0)
    payload_before = lax.ppermute(payload, "facet", facet_ring)

    depth = n * rows
    picture = jax.ShapeDtypeStruct((SUB, SUB), jnp.float32)
    scale = 1.0 / (2.0 * math.sqrt(n * rows))
    factor_rows = 2 * (4 * HALF + TILE + 2 * SUB)
    room = 24 + (2 * factor_rows * depth >> 20)

    def pictures_of(spilled, *operands):
        return pl.pallas_call(
            functools.partial(picture_kernel, n, scale, spilled),
            out_shape=(jax.ShapeDtypeStruct((2, SUB, SUB), jnp.float32), picture),
            in_specs=[vmem, vmem if spilled else anywhere, vmem, vmem]
            + [vmem] * (len(operands) - 4),
            out_specs=(vmem, vmem),
            scratch_shapes=[
                pltpu.SMEM((1, rows), jnp.float32),
                pltpu.VMEM((4 * HALF + 2 * TILE, depth), jnp.bfloat16),
                pltpu.VMEM((4 * HALF, depth), jnp.bfloat16),
                pltpu.VMEM((2 * SUB, depth), jnp.bfloat16),
                pltpu.VMEM((2 * SUB, depth), jnp.bfloat16),
                pltpu.SemaphoreType.DMA((1 + PARTS,)),
            ]
            + [pltpu.VMEM((2, SUB, SUB), jnp.float32)] * (not spilled),
            compiler_params=pltpu.CompilerParams(vmem_limit_bytes=max(room << 20, 0 if spilled else 209 << 18)),
            cost_estimate=pl.CostEstimate(
                flops=2 * depth * SUB * SUB * 4, bytes_accessed=4 << 20, transcendentals=0
            ),
        )(*operands)

    own, across = pictures_of(False, payload, screens, ahead, behind)
    before, across = pictures_of(True, payload_before, screens_before, ahead, behind, across)
    across = lax.ppermute(across, "chan", [(i, (i + 1) % n) for i in range(n)])
    image, block = pl.pallas_call(
        functools.partial(paste_kernel, n),
        out_shape=(jax.ShapeDtypeStruct((STRIP, BAND), jnp.float32), picture),
        in_specs=[anywhere] * 2 + [vmem] * 2,
        out_specs=(vmem, vmem),
        scratch_shapes=[pltpu.SMEM((2, rows), jnp.float32), pltpu.SemaphoreType.DMA((2,))],
        compiler_params=pltpu.CompilerParams(vmem_limit_bytes=16 << 20),
        cost_estimate=pl.CostEstimate(flops=1 << 20, bytes_accessed=12 << 20, transcendentals=0),
    )(payload, payload_before, own, before)
    return pl.pallas_call(
        finish_kernel,
        out_shape=jax.ShapeDtypeStruct((STRIP, BAND), jnp.float32),
        in_specs=[anywhere, vmem, vmem],
        out_specs=anywhere,
        scratch_shapes=[pltpu.VMEM((STRIP, SUB), jnp.float32), pltpu.SemaphoreType.DMA],
        input_output_aliases={0: 0},
        compiler_params=pltpu.CompilerParams(vmem_limit_bytes=4 << 20),
    )(image, block, across)


def solution(mesh):
    return jax.shard_map(
        functools.partial(shards, mesh),
        mesh=mesh,
        in_specs=(
            P("facet", "chan", None, None, None),
            P("facet", "chan", None, None, None),
            P("facet", "chan", None, None),
            P("facet", "chan", None),
            P("facet", "chan", None, None, None),
            P("facet", "chan", None, None),
        ),
        out_specs=P("facet", "chan"),
        check_vma=False,
    )
```

```python
import functools
import math

import jax
import jax.numpy as jnp
from jax import lax
from jax.experimental import pallas as pl
from jax.experimental.pallas import tpu as pltpu
from jax.sharding import PartitionSpec as P

TAPS = 8
STRIP = 256
BAND = 4096
SUB = 256
HALF = SUB // 2
BLOCK = 64
TILE = 16
LAST = BAND // SUB - 1
PARTS = 8


def numbers_kernel(n, tracks, counts, offsets, out):
    me = lax.axis_index("chan")
    lane = lax.broadcasted_iota(jnp.int32, (1, out.shape[1]), 1)
    block = lane // BLOCK
    lines = []
    for k in range(n):
        source = sender(n, me, k)
        target = jnp.zeros_like(lane)
        for b in range(tracks.shape[-1]):
            target = jnp.where(block == b, tracks[0, 0, source, b], target)
        lines += [target, jnp.where(block < counts[0, 0, source], 1, 0)]
    corners = jnp.zeros_like(lane)
    for place in range(4):
        corners = jnp.where(lane == place, offsets[0, 0, place // 2, place % 2], corners)
    lines += [corners] * (out.shape[0] - 2 * n)
    out[...] = jnp.concatenate(lines, axis=0).astype(jnp.float32)


def tables_kernel(numbers_in, ahead, behind, numbers):
    numbers[...] = numbers_in[...]
    shape = (SUB, SUB)
    for across, out in ((1, ahead), (0, behind)):
        j = lax.broadcasted_iota(jnp.int32, shape, across)
        x = lax.broadcasted_iota(jnp.int32, shape, 1 - across)
        turn = jnp.where(j > HALF, (j - HALF) * x + 3 * SUB // 4, j * x) & (SUB - 1)
        turn = jnp.minimum(turn, SUB - turn).astype(jnp.float32)
        half_angle = cosine(turn * (math.pi / SUB))
        high, low = halves(2.0 * half_angle * half_angle - 1.0)
        out[:SUB] = high
        out[SUB:] = low


def halves(value):
    high = value.astype(jnp.bfloat16)
    low = (value - high.astype(jnp.float32)).astype(jnp.bfloat16)
    return high, low


def cosine(angle):
    square = angle * angle
    series = jnp.float32(-1.0 / math.factorial(14))
    for order in range(12, -1, -2):
        sign = 1.0 if order % 4 == 0 else -1.0
        series = series * square + jnp.float32(sign / math.factorial(order))
    return series


def taper(offset):
    series = cosine(offset * (math.pi / TAPS))
    return jnp.where(jnp.abs(offset) < TAPS / 2, series * series, 0.0)


def folded(position, rho):
    base = jnp.floor(position) - (TAPS // 2 - 1)

    def cell_at(residue):
        ahead = residue - base
        ahead = ahead - TILE * jnp.floor(ahead * (1.0 / TILE))
        return base + ahead, ahead < TAPS

    cell, inside = cell_at(rho)
    direct = inside & (cell <= HALF)
    near = jnp.where(direct, taper(cell - position), 0.0)
    mirror, inside = cell_at(-rho)
    far = jnp.where(inside & (mirror > HALF), taper(mirror - position), 0.0)
    turn = jnp.where(direct, cell - rho, SUB - mirror - rho) * (1.0 / TILE)
    return near + far, near - far, turn.astype(jnp.bfloat16)


def sender(n, me, k):
    return me ^ (0, 2, 1, 3)[k] if n == 4 else lax.rem(me - k + n, n)


def exchange(n, me, visibilities, positions, numbers):
    def slot(index):
        parts = [lax.dynamic_index_in_dim(a[0, 0], index, 0, False) for a in (visibilities, positions)]
        return jnp.concatenate(parts, axis=0)

    def swap(piece, bit):
        return lax.ppermute(piece, "chan", [(i, i ^ bit) for i in range(n)])

    if n != 4:
        pieces = [slot(me)]
        for k in range(1, n):
            ring = [(i, (i + k) % n) for i in range(n)]
            pieces.append(lax.ppermute(slot(lax.rem(me + k, n)), "chan", ring))
        return pieces
    far = swap(jnp.concatenate([slot(me ^ 2), slot(me ^ 3)], axis=0), 2)
    far, numbers = lax.optimization_barrier((far, numbers))
    near = swap(jnp.concatenate([slot(me ^ 1), far[4:]], axis=0), 1)
    return [slot(me), far[:4], near]


def fill_factors(n, payload, le, lo, we, wo):
    rows = payload.shape[-1]
    rho = lax.broadcasted_iota(jnp.int32, (TILE, rows), 0).astype(jnp.float32)
    zero = jnp.zeros((TILE, rows), jnp.bfloat16)
    for k in range(n):
        piece = payload[4 * k : 4 * k + 4]
        target = payload[4 * n + 2 * k : 4 * n + 2 * k + 1]
        live = payload[4 * n + 2 * k + 1 : 4 * n + 2 * k + 2]
        real = piece[0:1] * live
        imag = piece[1:2] * live
        u_position = piece[2:3]
        u_even, u_odd, u_turn = folded(u_position, rho)
        v_even, v_odd, v_turn = folded(piece[3:4], rho)
        middle = taper(HALF - u_position)
        place = pl.ds(k * rows, rows)

        def put(ref, row, pair):
            for part, value in enumerate(pair):
                start = part * (ref.shape[0] // 2) + row
                ref[start : start + TILE, place] = value

        first = target == 0.0
        evens = [halves(jnp.where(first, u_even, 0.0)), halves(jnp.where(first, 0.0, u_even))]
        odds = [halves(jnp.where(first, u_odd, 0.0)), halves(jnp.where(first, 0.0, u_odd))]
        for turn in range(HALF // TILE):
            chosen = u_turn == turn
            for s in range(2):
                row = s * HALF + turn * TILE
                put(le, row, [jnp.where(chosen, e, zero) for e in evens[s]])
                put(lo, row, [jnp.where(chosen, o, zero) for o in odds[s]])
        middles = jnp.where(
            (rho == 0) & first, middle, jnp.where((rho == 8) & jnp.logical_not(first), middle, 0.0)
        )
        put(le, 2 * HALF, halves(middles))
        for ref, cosine, sine in (
            (we, real * v_even, imag * v_odd),
            (wo, imag * v_even, -real * v_odd),
        ):
            cosine, sine = halves(cosine), halves(sine)
            for turn in range(HALF // TILE):
                chosen = v_turn == turn
                put(ref, turn * TILE, [jnp.where(chosen, c, zero) for c in cosine])
                pair = [jnp.where(chosen, c, zero) for c in sine]
                if turn == 0:
                    top = v_turn == HALF // TILE
                    pair = [jnp.where(top, c, p) for c, p in zip(cosine, pair)]
                put(ref, HALF + turn * TILE, pair)


def product(a, b, contract):
    rows, half = a.shape[0] // 2, b.shape[0] // 2

    def dot(left, right):
        numbers = (((1,), (contract,)), ((), ()))
        return lax.dot_general(left, right, numbers, preferred_element_type=jnp.float32)

    main = dot(a, b[:half])
    return main[:rows] + main[rows:] + dot(a[:rows], b[half:])


def picture_kernel(n, scale, turn, *refs):
    if turn < 2:

        @pl.when(lax.rem(lax.axis_index("facet"), 2) == 1 - turn)
        def _():
            make_pictures(n, scale, False, *refs)

    else:
        make_pictures(n, scale, True, *refs)


def own_part(first, second):
    return jnp.where(lax.rem(lax.axis_index("facet"), 2) == 1, first, second)


def make_pictures(n, scale, spilled, *refs):
    count = 6 if spilled else 4
    payload, screens_in, ahead, behind = refs[:4]
    pictures, across = refs[count : count + 2]
    corners, le, lo, we, wo, sems = refs[count + 2 : count + 8]
    copies = [pltpu.make_async_copy(payload.at[pl.ds(6 * n, 1)], corners, sems.at[0])]
    if spilled:
        screens = screens_in.at[0, 0]
    else:
        screens = refs[-1]
        for part in range(PARTS):
            place = (part * 2 // PARTS, pl.ds(part % (PARTS // 2) * (2 * SUB // PARTS), 2 * SUB // PARTS))
            copies.append(
                pltpu.make_async_copy(
                    screens_in.at[0, 0].at[place], screens.at[place], sems.at[1 + part]
                )
            )
    for copy in copies:
        copy.start()
    fill_factors(n, payload, le, lo, we, wo)
    even = product(le[...], we[...], 1)
    odd = product(lo[...], wo[...], 1)
    row_ids = lax.broadcasted_iota(jnp.int32, (SUB, SUB), 0)
    col_ids = lax.broadcasted_iota(jnp.int32, (SUB, SUB), 1)
    first_row = lax.broadcasted_iota(jnp.int32, (HALF, SUB), 0) == 0
    total = own_part(refs[4][...], refs[5][...]) if spilled else jnp.zeros((SUB, SUB), jnp.float32)
    grids = []
    for s in range(2):
        middle = even[2 * HALF + 8 * s : 2 * HALF + 8 * s + 1]
        lower = jnp.where(first_row, middle, odd[s * HALF : (s + 1) * HALF])
        grids += [even[s * HALF : (s + 1) * HALF], lower]
    half_way = product(
        jnp.concatenate(halves(jnp.concatenate(grids, axis=0)), axis=0), behind[...], 0
    )
    for s in range(2):
        image = jnp.concatenate(halves(half_way[s * SUB : (s + 1) * SUB]), axis=0)
        image = product(ahead[...], image, 0)
        if s == 0:
            copies[0].wait()
        for copy in copies[1 + s * PARTS // 2 : 1 + (s + 1) * PARTS // 2]:
            copy.wait()
        image = screens[s] * (image * scale)
        row = corners[0, 2 * s].astype(jnp.int32)
        col = corners[0, 2 * s + 1].astype(jnp.int32)
        shift = lax.rem(col, SUB)
        image = pltpu.roll(pltpu.roll(image, row, 0), shift, 1)
        here = (row_ids < row) if spilled else (row_ids >= row)
        image = jnp.where(here, image, 0.0)
        pictures[s] = image
        beyond = (col_ids < shift) & (col // SUB == LAST)
        total = total + jnp.where(beyond, image, 0.0)
    across[...] = total


def paste_kernel(n, payload_in, payload_before, own, own_later, before, out, block_out, corners, sems):
    copies = [
        pltpu.make_async_copy(source.at[pl.ds(6 * n, 1)], corners.at[pl.ds(i, 1)], sems.at[i])
        for i, source in enumerate((payload_in, payload_before))
    ]
    for copy in copies:
        copy.start()
    out[...] = jnp.zeros_like(out)
    for copy in copies:
        copy.wait()
    col_ids = lax.broadcasted_iota(jnp.int32, (SUB, SUB), 1)
    for i, pictures in enumerate((own, before)):
        for s in range(2):
            col = corners[i, 2 * s + 1].astype(jnp.int32)
            shift = lax.rem(col, SUB)
            block = col // SUB
            image = pictures[s] if i else own_part(own[s], own_later[s])
            place = pl.ds(pl.multiple_of(block * SUB, SUB), SUB)
            out[:, place] += jnp.where(col_ids >= shift, image, 0.0)

            @pl.when(block < LAST)
            def _():
                place = pl.ds(pl.multiple_of((block + 1) * SUB, SUB), SUB)
                out[:, place] += jnp.where(col_ids < shift, image, 0.0)

    block_out[...] = out[:, :SUB]


def finish_kernel(image_in, block, across, image_out, total, sem):
    total[...] = block[...] + across[...]
    copy = pltpu.make_async_copy(total, image_out.at[:, pl.ds(0, SUB)], sem)
    copy.start()
    copy.wait()


def shards(mesh, visibilities, positions, tracks, counts, screens, offsets):
    n = mesh.shape["chan"]
    facets = mesh.shape["facet"]
    rows = visibilities.shape[-1]
    vmem = pl.BlockSpec(memory_space=pltpu.VMEM)
    anywhere = pl.BlockSpec(memory_space=pl.ANY)
    hbm = pl.BlockSpec(memory_space=pltpu.HBM)
    facet_ring = [(i, (i + 1) % facets) for i in range(facets)]

    numbers = pl.pallas_call(
        functools.partial(numbers_kernel, n),
        out_shape=jax.ShapeDtypeStruct((2 * n + 8, rows), jnp.float32),
        in_specs=[pl.BlockSpec(memory_space=pltpu.SMEM)] * 3,
        out_specs=vmem,
        compiler_params=pltpu.CompilerParams(vmem_limit_bytes=56 << 20),
    )(tracks, counts, offsets)
    pieces = exchange(n, lax.axis_index("chan"), visibilities, positions, numbers)
    screens_before = lax.ppermute(screens, "facet", facet_ring)
    ahead, behind, numbers = pl.pallas_call(
        tables_kernel,
        out_shape=(
            jax.ShapeDtypeStruct((2 * SUB, SUB), jnp.bfloat16),
            jax.ShapeDtypeStruct((2 * SUB, SUB), jnp.bfloat16),
            jax.ShapeDtypeStruct((2 * n + 8, rows), jnp.float32),
        ),
        in_specs=[vmem],
        out_specs=(vmem, vmem, vmem),
        compiler_params=pltpu.CompilerParams(vmem_limit_bytes=8 << 20),
        cost_estimate=pl.CostEstimate(flops=4 << 20, bytes_accessed=1 << 20, transcendentals=0),
    )(numbers)
    payload = jnp.concatenate(pieces + [numbers], axis=0)

    depth = n * rows
    picture = jax.ShapeDtypeStruct((SUB, SUB), jnp.float32)
    scale = 1.0 / (2.0 * math.sqrt(n * rows))
    factor_rows = 2 * (4 * HALF + TILE + 2 * SUB)
    room = 24 + (2 * factor_rows * depth >> 20)

    def pictures_of(turn, *operands):
        spilled = turn == 2
        return pl.pallas_call(
            functools.partial(picture_kernel, n, scale, turn),
            out_shape=(jax.ShapeDtypeStruct((2, SUB, SUB), jnp.float32), picture),
            in_specs=[vmem, vmem if spilled else anywhere, vmem, vmem]
            + [vmem] * (len(operands) - 4),
            out_specs=(vmem, vmem),
            scratch_shapes=[
                pltpu.SMEM((1, rows), jnp.float32),
                pltpu.VMEM((4 * HALF + 2 * TILE, depth), jnp.bfloat16),
                pltpu.VMEM((4 * HALF, depth), jnp.bfloat16),
                pltpu.VMEM((2 * SUB, depth), jnp.bfloat16),
                pltpu.VMEM((2 * SUB, depth), jnp.bfloat16),
                pltpu.SemaphoreType.DMA((1 + PARTS,)),
            ]
            + [pltpu.VMEM((2, SUB, SUB), jnp.float32)] * (not spilled),
            compiler_params=pltpu.CompilerParams(vmem_limit_bytes=max(room << 20, 0 if spilled else 209 << 18)),
            cost_estimate=pl.CostEstimate(
                flops=2 * depth * SUB * SUB * 4, bytes_accessed=4 << 20, transcendentals=0
            ),
        )(*operands)

    own, across = pictures_of(0, payload, screens, ahead, behind)
    payload, across = lax.optimization_barrier((payload, across))
    payload_before = lax.ppermute(payload, "facet", facet_ring)
    own_later, across_later = pictures_of(1, payload, screens, ahead, behind)
    before, across = pictures_of(
        2, payload_before, screens_before, ahead, behind, across, across_later
    )
    across = lax.ppermute(across, "chan", [(i, (i + 1) % n) for i in range(n)])
    image, block = pl.pallas_call(
        functools.partial(paste_kernel, n),
        out_shape=(jax.ShapeDtypeStruct((STRIP, BAND), jnp.float32), picture),
        in_specs=[anywhere] * 2 + [vmem] * 3,
        out_specs=(vmem, vmem),
        scratch_shapes=[pltpu.SMEM((2, rows), jnp.float32), pltpu.SemaphoreType.DMA((2,))],
        compiler_params=pltpu.CompilerParams(vmem_limit_bytes=16 << 20),
        cost_estimate=pl.CostEstimate(flops=1 << 20, bytes_accessed=12 << 20, transcendentals=0),
    )(payload, payload_before, own, own_later, before)
    return pl.pallas_call(
        finish_kernel,
        out_shape=jax.ShapeDtypeStruct((STRIP, BAND), jnp.float32),
        in_specs=[anywhere, vmem, vmem],
        out_specs=anywhere,
        scratch_shapes=[pltpu.VMEM((STRIP, SUB), jnp.float32), pltpu.SemaphoreType.DMA],
        input_output_aliases={0: 0},
        compiler_params=pltpu.CompilerParams(vmem_limit_bytes=4 << 20),
    )(image, block, across)


def solution(mesh):
    return jax.shard_map(
        functools.partial(shards, mesh),
        mesh=mesh,
        in_specs=(
            P("facet", "chan", None, None, None),
            P("facet", "chan", None, None, None),
            P("facet", "chan", None, None),
            P("facet", "chan", None),
            P("facet", "chan", None, None, None),
            P("facet", "chan", None, None),
        ),
        out_specs=P("facet", "chan"),
        check_vma=False,
    )
```

```python
import functools
import math

import jax
import jax.numpy as jnp
from jax import lax
from jax.experimental import pallas as pl
from jax.experimental.pallas import tpu as pltpu
from jax.sharding import PartitionSpec as P

TAPS = 8
STRIP = 256
BAND = 4096
SUB = 256
HALF = SUB // 2
BLOCK = 64
TILE = 16
LAST = BAND // SUB - 1
PARTS = 8


def numbers_kernel(n, tracks, counts, offsets, out):
    me = lax.axis_index("chan")
    lane = lax.broadcasted_iota(jnp.int32, (1, out.shape[1]), 1)
    block = lane // BLOCK
    lines = []
    for k in range(n):
        source = sender(n, me, k)
        target = jnp.zeros_like(lane)
        for b in range(tracks.shape[-1]):
            target = jnp.where(block == b, tracks[0, 0, source, b], target)
        lines += [target, jnp.where(block < counts[0, 0, source], 1, 0)]
    corners = jnp.zeros_like(lane)
    for place in range(4):
        corners = jnp.where(lane == place, offsets[0, 0, place // 2, place % 2], corners)
    lines += [corners] * (out.shape[0] - 2 * n)
    out[...] = jnp.concatenate(lines, axis=0).astype(jnp.float32)


def tables_kernel(numbers_in, ahead, behind, numbers):
    numbers[...] = numbers_in[...]
    shape = (SUB, SUB)
    for across, out in ((1, ahead), (0, behind)):
        j = lax.broadcasted_iota(jnp.int32, shape, across)
        x = lax.broadcasted_iota(jnp.int32, shape, 1 - across)
        turn = jnp.where(j > HALF, (j - HALF) * x + 3 * SUB // 4, j * x) & (SUB - 1)
        turn = jnp.minimum(turn, SUB - turn).astype(jnp.float32)
        half_angle = cosine(turn * (math.pi / SUB))
        high, low = halves(2.0 * half_angle * half_angle - 1.0)
        out[:SUB] = high
        out[SUB:] = low


def halves(value):
    high = value.astype(jnp.bfloat16)
    low = (value - high.astype(jnp.float32)).astype(jnp.bfloat16)
    return high, low


def cosine(angle):
    square = angle * angle
    series = jnp.float32(-1.0 / math.factorial(14))
    for order in range(12, -1, -2):
        sign = 1.0 if order % 4 == 0 else -1.0
        series = series * square + jnp.float32(sign / math.factorial(order))
    return series


def taper(offset):
    series = cosine(offset * (math.pi / TAPS))
    return jnp.where(jnp.abs(offset) < TAPS / 2, series * series, 0.0)


def folded(position, rho):
    base = jnp.floor(position) - (TAPS // 2 - 1)

    def cell_at(residue):
        ahead = residue - base
        ahead = ahead - TILE * jnp.floor(ahead * (1.0 / TILE))
        return base + ahead, ahead < TAPS

    cell, inside = cell_at(rho)
    direct = inside & (cell <= HALF)
    near = jnp.where(direct, taper(cell - position), 0.0)
    mirror, inside = cell_at(-rho)
    far = jnp.where(inside & (mirror > HALF), taper(mirror - position), 0.0)
    turn = jnp.where(direct, cell - rho, SUB - mirror - rho) * (1.0 / TILE)
    return near + far, near - far, turn.astype(jnp.bfloat16)


def sender(n, me, k):
    return me ^ k if n == 4 else lax.rem(me - k + n, n)


def exchange(n, me, visibilities, positions, numbers):
    def slot(index):
        parts = [lax.dynamic_index_in_dim(a[0, 0], index, 0, False) for a in (visibilities, positions)]
        return jnp.concatenate(parts, axis=0)

    def swap(piece, bit):
        return lax.ppermute(piece, "chan", [(i, i ^ bit) for i in range(n)])

    if n != 4:
        pieces = [slot(me)]
        for k in range(1, n):
            ring = [(i, (i + k) % n) for i in range(n)]
            pieces.append(lax.ppermute(slot(lax.rem(me + k, n)), "chan", ring))
        return pieces
    near = swap(jnp.concatenate([slot(me ^ 1), slot(me ^ 3)], axis=0), 1)
    near, numbers = lax.optimization_barrier((near, numbers))
    far = swap(jnp.concatenate([slot(me ^ 2), near[4:]], axis=0), 2)
    return [slot(me), near[:4], far]


def fill_factors(n, payload, le, lo, we, wo):
    rows = payload.shape[-1]
    rho = lax.broadcasted_iota(jnp.int32, (TILE, rows), 0).astype(jnp.float32)
    zero = jnp.zeros((TILE, rows), jnp.bfloat16)
    for k in range(n):
        piece = payload[4 * k : 4 * k + 4]
        target = payload[4 * n + 2 * k : 4 * n + 2 * k + 1]
        live = payload[4 * n + 2 * k + 1 : 4 * n + 2 * k + 2]
        real = piece[0:1] * live
        imag = piece[1:2] * live
        u_position = piece[2:3]
        u_even, u_odd, u_turn = folded(u_position, rho)
        v_even, v_odd, v_turn = folded(piece[3:4], rho)
        middle = taper(HALF - u_position)
        place = pl.ds(k * rows, rows)

        def put(ref, row, pair):
            for part, value in enumerate(pair):
                start = part * (ref.shape[0] // 2) + row
                ref[start : start + TILE, place] = value

        first = target == 0.0
        evens = [halves(jnp.where(first, u_even, 0.0)), halves(jnp.where(first, 0.0, u_even))]
        odds = [halves(jnp.where(first, u_odd, 0.0)), halves(jnp.where(first, 0.0, u_odd))]
        for turn in range(HALF // TILE):
            chosen = u_turn == turn
            for s in range(2):
                row = s * HALF + turn * TILE
                put(le, row, [jnp.where(chosen, e, zero) for e in evens[s]])
                put(lo, row, [jnp.where(chosen, o, zero) for o in odds[s]])
        middles = jnp.where(
            (rho == 0) & first, middle, jnp.where((rho == 8) & jnp.logical_not(first), middle, 0.0)
        )
        put(le, 2 * HALF, halves(middles))
        for ref, cosine, sine in (
            (we, real * v_even, imag * v_odd),
            (wo, imag * v_even, -real * v_odd),
        ):
            cosine, sine = halves(cosine), halves(sine)
            for turn in range(HALF // TILE):
                chosen = v_turn == turn
                put(ref, turn * TILE, [jnp.where(chosen, c, zero) for c in cosine])
                pair = [jnp.where(chosen, c, zero) for c in sine]
                if turn == 0:
                    top = v_turn == HALF // TILE
                    pair = [jnp.where(top, c, p) for c, p in zip(cosine, pair)]
                put(ref, HALF + turn * TILE, pair)


def product(a, b, contract):
    rows, half = a.shape[0] // 2, b.shape[0] // 2

    def dot(left, right):
        numbers = (((1,), (contract,)), ((), ()))
        return lax.dot_general(left, right, numbers, preferred_element_type=jnp.float32)

    main = dot(a, b[:half])
    return main[:rows] + main[rows:] + dot(a[:rows], b[half:])


def picture_kernel(n, scale, turn, *refs):
    if turn < 2:

        @pl.when(lax.rem(lax.axis_index("facet"), 2) == 1 - turn)
        def _():
            make_pictures(n, scale, False, *refs)

    else:
        make_pictures(n, scale, True, *refs)


def own_part(first, second):
    return jnp.where(lax.rem(lax.axis_index("facet"), 2) == 1, first, second)


def make_pictures(n, scale, spilled, *refs):
    count = 6 if spilled else 4
    payload, screens_in, ahead, behind = refs[:4]
    pictures, across = refs[count : count + 2]
    corners, le, lo, we, wo, sems = refs[count + 2 : count + 8]
    copies = [pltpu.make_async_copy(payload.at[pl.ds(6 * n, 1)], corners, sems.at[0])]
    if spilled:
        screens = screens_in.at[0, 0]
    else:
        screens = refs[-1]
        for part in range(PARTS):
            place = (part * 2 // PARTS, pl.ds(part % (PARTS // 2) * (2 * SUB // PARTS), 2 * SUB // PARTS))
            copies.append(
                pltpu.make_async_copy(
                    screens_in.at[0, 0].at[place], screens.at[place], sems.at[1 + part]
                )
            )
    for copy in copies:
        copy.start()
    fill_factors(n, payload, le, lo, we, wo)
    even = product(le[...], we[...], 1)
    odd = product(lo[...], wo[...], 1)
    row_ids = lax.broadcasted_iota(jnp.int32, (SUB, SUB), 0)
    col_ids = lax.broadcasted_iota(jnp.int32, (SUB, SUB), 1)
    first_row = lax.broadcasted_iota(jnp.int32, (HALF, SUB), 0) == 0
    total = own_part(refs[4][...], refs[5][...]) if spilled else jnp.zeros((SUB, SUB), jnp.float32)
    grids = []
    for s in range(2):
        middle = even[2 * HALF + 8 * s : 2 * HALF + 8 * s + 1]
        lower = jnp.where(first_row, middle, odd[s * HALF : (s + 1) * HALF])
        grids += [even[s * HALF : (s + 1) * HALF], lower]
    half_way = product(
        jnp.concatenate(halves(jnp.concatenate(grids, axis=0)), axis=0), behind[...], 0
    )
    for s in range(2):
        image = jnp.concatenate(halves(half_way[s * SUB : (s + 1) * SUB]), axis=0)
        image = product(ahead[...], image, 0)
        if s == 0:
            copies[0].wait()
        for copy in copies[1 + s * PARTS // 2 : 1 + (s + 1) * PARTS // 2]:
            copy.wait()
        image = screens[s] * (image * scale)
        row = corners[0, 2 * s].astype(jnp.int32)
        col = corners[0, 2 * s + 1].astype(jnp.int32)
        shift = lax.rem(col, SUB)
        image = pltpu.roll(pltpu.roll(image, row, 0), shift, 1)
        here = (row_ids < row) if spilled else (row_ids >= row)
        image = jnp.where(here, image, 0.0)
        pictures[s] = image
        beyond = (col_ids < shift) & (col // SUB == LAST)
        total = total + jnp.where(beyond, image, 0.0)
    across[...] = total


def paste_kernel(n, payload_in, payload_before, own, own_later, before, out, block_out, corners, sems):
    copies = [
        pltpu.make_async_copy(source.at[pl.ds(6 * n, 1)], corners.at[pl.ds(i, 1)], sems.at[i])
        for i, source in enumerate((payload_in, payload_before))
    ]
    for copy in copies:
        copy.start()
    out[...] = jnp.zeros_like(out)
    for copy in copies:
        copy.wait()
    col_ids = lax.broadcasted_iota(jnp.int32, (SUB, SUB), 1)
    for i, pictures in enumerate((own, before)):
        for s in range(2):
            col = corners[i, 2 * s + 1].astype(jnp.int32)
            shift = lax.rem(col, SUB)
            block = col // SUB
            image = pictures[s] if i else own_part(own[s], own_later[s])
            place = pl.ds(pl.multiple_of(block * SUB, SUB), SUB)
            out[:, place] += jnp.where(col_ids >= shift, image, 0.0)

            @pl.when(block < LAST)
            def _():
                place = pl.ds(pl.multiple_of((block + 1) * SUB, SUB), SUB)
                out[:, place] += jnp.where(col_ids < shift, image, 0.0)

    block_out[...] = out[:, :SUB]


def finish_kernel(image_in, block, across, image_out, total, sem):
    total[...] = block[...] + across[...]
    copy = pltpu.make_async_copy(total, image_out.at[:, pl.ds(0, SUB)], sem)
    copy.start()
    copy.wait()


def shards(mesh, visibilities, positions, tracks, counts, screens, offsets):
    n = mesh.shape["chan"]
    facets = mesh.shape["facet"]
    rows = visibilities.shape[-1]
    vmem = pl.BlockSpec(memory_space=pltpu.VMEM)
    anywhere = pl.BlockSpec(memory_space=pl.ANY)
    facet_ring = [(i, (i + 1) % facets) for i in range(facets)]

    numbers = pl.pallas_call(
        functools.partial(numbers_kernel, n),
        out_shape=jax.ShapeDtypeStruct((2 * n + 8, rows), jnp.float32),
        in_specs=[pl.BlockSpec(memory_space=pltpu.SMEM)] * 3,
        out_specs=vmem,
        compiler_params=pltpu.CompilerParams(vmem_limit_bytes=56 << 20),
    )(tracks, counts, offsets)
    pieces = exchange(n, lax.axis_index("chan"), visibilities, positions, numbers)
    screens_before = lax.ppermute(screens, "facet", facet_ring)
    ahead, behind, numbers = pl.pallas_call(
        tables_kernel,
        out_shape=(
            jax.ShapeDtypeStruct((2 * SUB, SUB), jnp.bfloat16),
            jax.ShapeDtypeStruct((2 * SUB, SUB), jnp.bfloat16),
            jax.ShapeDtypeStruct((2 * n + 8, rows), jnp.float32),
        ),
        in_specs=[vmem],
        out_specs=(vmem, vmem, vmem),
        compiler_params=pltpu.CompilerParams(vmem_limit_bytes=8 << 20),
        cost_estimate=pl.CostEstimate(flops=4 << 20, bytes_accessed=1 << 20, transcendentals=0),
    )(numbers)
    payload = jnp.concatenate(pieces + [numbers], axis=0)

    depth = n * rows
    picture = jax.ShapeDtypeStruct((SUB, SUB), jnp.float32)
    scale = 1.0 / (2.0 * math.sqrt(n * rows))
    factor_rows = 2 * (4 * HALF + TILE + 2 * SUB)
    room = 24 + (2 * factor_rows * depth >> 20)

    def pictures_of(turn, *operands):
        spilled = turn == 2
        return pl.pallas_call(
            functools.partial(picture_kernel, n, scale, turn),
            out_shape=(jax.ShapeDtypeStruct((2, SUB, SUB), jnp.float32), picture),
            in_specs=[vmem, vmem if spilled else anywhere, vmem, vmem]
            + [vmem] * (len(operands) - 4),
            out_specs=(vmem, vmem),
            scratch_shapes=[
                pltpu.SMEM((1, rows), jnp.float32),
                pltpu.VMEM((4 * HALF + 2 * TILE, depth), jnp.bfloat16),
                pltpu.VMEM((4 * HALF, depth), jnp.bfloat16),
                pltpu.VMEM((2 * SUB, depth), jnp.bfloat16),
                pltpu.VMEM((2 * SUB, depth), jnp.bfloat16),
                pltpu.SemaphoreType.DMA((1 + PARTS,)),
            ]
            + [pltpu.VMEM((2, SUB, SUB), jnp.float32)] * (not spilled),
            compiler_params=pltpu.CompilerParams(
                vmem_limit_bytes=max(room << 20, 0 if spilled else 209 << 18)
            ),
            cost_estimate=pl.CostEstimate(
                flops=2 * depth * SUB * SUB * 4, bytes_accessed=4 << 20, transcendentals=0
            ),
        )(*operands)

    own, across = pictures_of(0, payload, screens, ahead, behind)
    payload, across = lax.optimization_barrier((payload, across))
    payload_before = lax.ppermute(payload, "facet", facet_ring)
    own_later, across_later = pictures_of(1, payload, screens, ahead, behind)
    before, across = pictures_of(
        2, payload_before, screens_before, ahead, behind, across, across_later
    )
    across = lax.ppermute(across, "chan", [(i, (i + 1) % n) for i in range(n)])
    image, block = pl.pallas_call(
        functools.partial(paste_kernel, n),
        out_shape=(jax.ShapeDtypeStruct((STRIP, BAND), jnp.float32), picture),
        in_specs=[anywhere] * 2 + [vmem] * 3,
        out_specs=(vmem, vmem),
        scratch_shapes=[pltpu.SMEM((2, rows), jnp.float32), pltpu.SemaphoreType.DMA((2,))],
        compiler_params=pltpu.CompilerParams(vmem_limit_bytes=16 << 20),
        cost_estimate=pl.CostEstimate(flops=1 << 20, bytes_accessed=12 << 20, transcendentals=0),
    )(payload, payload_before, own, own_later, before)
    return pl.pallas_call(
        finish_kernel,
        out_shape=jax.ShapeDtypeStruct((STRIP, BAND), jnp.float32),
        in_specs=[anywhere, vmem, vmem],
        out_specs=anywhere,
        scratch_shapes=[pltpu.VMEM((STRIP, SUB), jnp.float32), pltpu.SemaphoreType.DMA],
        input_output_aliases={0: 0},
        compiler_params=pltpu.CompilerParams(vmem_limit_bytes=4 << 20),
    )(image, block, across)


def solution(mesh):
    return jax.shard_map(
        functools.partial(shards, mesh),
        mesh=mesh,
        in_specs=(
            P("facet", "chan", None, None, None),
            P("facet", "chan", None, None, None),
            P("facet", "chan", None, None),
            P("facet", "chan", None),
            P("facet", "chan", None, None, None),
            P("facet", "chan", None, None),
        ),
        out_specs=P("facet", "chan"),
        check_vma=False,
    )
```

```python
import functools
import math

import jax
import jax.numpy as jnp
from jax import lax
from jax.experimental import pallas as pl
from jax.experimental.pallas import tpu as pltpu
from jax.sharding import PartitionSpec as P

TAPS = 8
STRIP = 256
BAND = 4096
SUB = 256
HALF = SUB // 2
BLOCK = 64
TILE = 16
LAST = BAND // SUB - 1
PARTS = 8


def numbers_kernel(n, tracks, counts, offsets, out):
    me = lax.axis_index("chan")
    lane = lax.broadcasted_iota(jnp.int32, (1, out.shape[1]), 1)
    block = lane // BLOCK
    lines = []
    for k in range(n):
        source = sender(n, me, k)
        target = jnp.zeros_like(lane)
        for b in range(tracks.shape[-1]):
            target = jnp.where(block == b, tracks[0, 0, source, b], target)
        lines.append(jnp.where(block < counts[0, 0, source], target + 1, 0))
    corners = jnp.zeros_like(lane)
    for place in range(4):
        corners = jnp.where(lane == place, offsets[0, 0, place // 2, place % 2], corners)
    lines = [corners] + lines + [corners] * (out.shape[0] - n - 1)
    out[...] = jnp.concatenate(lines, axis=0).astype(jnp.float32)


def tables_kernel(numbers_in, ahead, behind, numbers):
    numbers[...] = numbers_in[...]
    shape = (SUB, SUB)
    for across, out in ((1, ahead), (0, behind)):
        j = lax.broadcasted_iota(jnp.int32, shape, across)
        x = lax.broadcasted_iota(jnp.int32, shape, 1 - across)
        turn = jnp.where(j > HALF, (j - HALF) * x + 3 * SUB // 4, j * x) & (SUB - 1)
        turn = jnp.minimum(turn, SUB - turn).astype(jnp.float32)
        half_angle = cosine(turn * (math.pi / SUB))
        high, low = halves(2.0 * half_angle * half_angle - 1.0)
        out[:SUB] = high
        out[SUB:] = low


def halves(value):
    high = value.astype(jnp.bfloat16)
    low = (value - high.astype(jnp.float32)).astype(jnp.bfloat16)
    return high, low


def cosine(angle):
    square = angle * angle
    series = jnp.float32(-1.0 / math.factorial(14))
    for order in range(12, -1, -2):
        sign = 1.0 if order % 4 == 0 else -1.0
        series = series * square + jnp.float32(sign / math.factorial(order))
    return series


def taper(offset):
    series = cosine(offset * (math.pi / TAPS))
    return jnp.where(jnp.abs(offset) < TAPS / 2, series * series, 0.0)


def folded(position, rho):
    base = jnp.floor(position) - (TAPS // 2 - 1)

    def cell_at(residue):
        ahead = residue - base
        ahead = ahead - TILE * jnp.floor(ahead * (1.0 / TILE))
        return base + ahead, ahead < TAPS

    cell, inside = cell_at(rho)
    direct = inside & (cell <= HALF)
    near = jnp.where(direct, taper(cell - position), 0.0)
    mirror, inside = cell_at(-rho)
    far = jnp.where(inside & (mirror > HALF), taper(mirror - position), 0.0)
    turn = jnp.where(direct, cell - rho, SUB - mirror - rho) * (1.0 / TILE)
    return near + far, near - far, turn.astype(jnp.bfloat16)


def sender(n, me, k):
    return me ^ k if n == 4 else lax.rem(me - k + n, n)


def exchange(n, me, visibilities, positions, numbers):
    def slot(index):
        parts = [lax.dynamic_index_in_dim(a[0, 0], index, 0, False) for a in (visibilities, positions)]
        return jnp.concatenate(parts, axis=0)

    def swap(piece, bit):
        return lax.ppermute(piece, "chan", [(i, i ^ bit) for i in range(n)])

    if n != 4:
        pieces = [slot(me)]
        for k in range(1, n):
            ring = [(i, (i + k) % n) for i in range(n)]
            pieces.append(lax.ppermute(slot(lax.rem(me + k, n)), "chan", ring))
        return pieces
    near = swap(jnp.concatenate([slot(me ^ 1), slot(me ^ 3)], axis=0), 1)
    near, numbers = lax.optimization_barrier((near, numbers))
    far = swap(jnp.concatenate([slot(me ^ 2), near[4:]], axis=0), 2)
    return [slot(me), near[:4], far]


def fill_factors(n, payload, le, lo, we, wo):
    rows = payload.shape[-1]
    rho = lax.broadcasted_iota(jnp.int32, (TILE, rows), 0).astype(jnp.float32)
    zero = jnp.zeros((TILE, rows), jnp.bfloat16)
    for k in range(n):
        piece = payload[4 * k : 4 * k + 4]
        target = payload[4 * n + 1 + k : 4 * n + 2 + k]
        real = jnp.where(target > 0.0, piece[0:1], 0.0)
        imag = jnp.where(target > 0.0, piece[1:2], 0.0)
        u_position = piece[2:3]
        u_even, u_odd, u_turn = folded(u_position, rho)
        v_even, v_odd, v_turn = folded(piece[3:4], rho)
        middle = taper(HALF - u_position)
        place = pl.ds(k * rows, rows)

        def put(ref, row, pair):
            for part, value in enumerate(pair):
                start = part * (ref.shape[0] // 2) + row
                ref[start : start + TILE, place] = value

        first = target < 2.0
        evens = [halves(jnp.where(first, u_even, 0.0)), halves(jnp.where(first, 0.0, u_even))]
        odds = [halves(jnp.where(first, u_odd, 0.0)), halves(jnp.where(first, 0.0, u_odd))]
        for turn in range(HALF // TILE):
            chosen = u_turn == turn
            for s in range(2):
                row = s * HALF + turn * TILE
                put(le, row, [jnp.where(chosen, e, zero) for e in evens[s]])
                put(lo, row, [jnp.where(chosen, o, zero) for o in odds[s]])
        middles = jnp.where(
            (rho == 0) & first, middle, jnp.where((rho == 8) & jnp.logical_not(first), middle, 0.0)
        )
        put(le, 2 * HALF, halves(middles))
        for ref, cosine, sine in (
            (we, real * v_even, imag * v_odd),
            (wo, imag * v_even, -real * v_odd),
        ):
            cosine, sine = halves(cosine), halves(sine)
            for turn in range(HALF // TILE):
                chosen = v_turn == turn
                put(ref, turn * TILE, [jnp.where(chosen, c, zero) for c in cosine])
                pair = [jnp.where(chosen, c, zero) for c in sine]
                if turn == 0:
                    top = v_turn == HALF // TILE
                    pair = [jnp.where(top, c, p) for c, p in zip(cosine, pair)]
                put(ref, HALF + turn * TILE, pair)


def product(a, b, contract):
    rows, half = a.shape[0] // 2, b.shape[0] // 2

    def dot(left, right):
        numbers = (((1,), (contract,)), ((), ()))
        return lax.dot_general(left, right, numbers, preferred_element_type=jnp.float32)

    main = dot(a, b[:half])
    return main[:rows] + main[rows:] + dot(a[:rows], b[half:])


def picture_kernel(n, scale, turn, *refs):
    if turn < 2:

        @pl.when(lax.rem(lax.axis_index("facet"), 2) == 1 - turn)
        def _():
            make_pictures(n, scale, False, *refs)

    else:
        make_pictures(n, scale, True, *refs)


def own_part(first, second):
    return jnp.where(lax.rem(lax.axis_index("facet"), 2) == 1, first, second)


def make_pictures(n, scale, spilled, *refs):
    count = 6 if spilled else 4
    payload, screens_in, ahead, behind = refs[:4]
    pictures, across = refs[count : count + 2]
    corners, le, lo, we, wo, sems = refs[count + 2 : count + 8]
    copies = [pltpu.make_async_copy(payload.at[pl.ds(4 * n, 1)], corners, sems.at[0])]
    if spilled:
        screens = screens_in.at[0, 0]
    else:
        screens = refs[-1]
        for part in range(PARTS):
            place = (part * 2 // PARTS, pl.ds(part % (PARTS // 2) * (2 * SUB // PARTS), 2 * SUB // PARTS))
            copies.append(
                pltpu.make_async_copy(
                    screens_in.at[0, 0].at[place], screens.at[place], sems.at[1 + part]
                )
            )
    for copy in copies:
        copy.start()
    fill_factors(n, payload, le, lo, we, wo)
    even = product(le[...], we[...], 1)
    odd = product(lo[...], wo[...], 1)
    row_ids = lax.broadcasted_iota(jnp.int32, (SUB, SUB), 0)
    col_ids = lax.broadcasted_iota(jnp.int32, (SUB, SUB), 1)
    first_row = lax.broadcasted_iota(jnp.int32, (HALF, SUB), 0) == 0
    total = own_part(refs[4][...], refs[5][...]) if spilled else jnp.zeros((SUB, SUB), jnp.float32)
    grids = []
    for s in range(2):
        middle = even[2 * HALF + 8 * s : 2 * HALF + 8 * s + 1]
        lower = jnp.where(first_row, middle, odd[s * HALF : (s + 1) * HALF])
        grids += [even[s * HALF : (s + 1) * HALF], lower]
    half_way = product(
        jnp.concatenate(halves(jnp.concatenate(grids, axis=0)), axis=0), behind[...], 0
    )
    for s in range(2):
        image = jnp.concatenate(halves(half_way[s * SUB : (s + 1) * SUB]), axis=0)
        image = product(ahead[...], image, 0)
        if s == 0:
            copies[0].wait()
        for copy in copies[1 + s * PARTS // 2 : 1 + (s + 1) * PARTS // 2]:
            copy.wait()
        image = screens[s] * (image * scale)
        row = corners[0, 2 * s].astype(jnp.int32)
        col = corners[0, 2 * s + 1].astype(jnp.int32)
        shift = lax.rem(col, SUB)
        image = pltpu.roll(pltpu.roll(image, row, 0), shift, 1)
        here = (row_ids < row) if spilled else (row_ids >= row)
        image = jnp.where(here, image, 0.0)
        pictures[s] = image
        beyond = (col_ids < shift) & (col // SUB == LAST)
        total = total + jnp.where(beyond, image, 0.0)
    across[...] = total


def paste_kernel(n, payload_in, payload_before, own, own_later, before, out, block_out, corners, sems):
    copies = [
        pltpu.make_async_copy(source.at[pl.ds(4 * n, 1)], corners.at[pl.ds(i, 1)], sems.at[i])
        for i, source in enumerate((payload_in, payload_before))
    ]
    for copy in copies:
        copy.start()
    out[...] = jnp.zeros_like(out)
    for copy in copies:
        copy.wait()
    col_ids = lax.broadcasted_iota(jnp.int32, (SUB, SUB), 1)
    for i, pictures in enumerate((own, before)):
        for s in range(2):
            col = corners[i, 2 * s + 1].astype(jnp.int32)
            shift = lax.rem(col, SUB)
            block = col // SUB
            image = pictures[s] if i else own_part(own[s], own_later[s])
            place = pl.ds(pl.multiple_of(block * SUB, SUB), SUB)
            out[:, place] += jnp.where(col_ids >= shift, image, 0.0)

            @pl.when(block < LAST)
            def _():
                place = pl.ds(pl.multiple_of((block + 1) * SUB, SUB), SUB)
                out[:, place] += jnp.where(col_ids < shift, image, 0.0)

    block_out[...] = out[:, :SUB]


def finish_kernel(image_in, block, across, image_out, total, sem):
    total[...] = block[...] + across[...]
    copy = pltpu.make_async_copy(total, image_out.at[:, pl.ds(0, SUB)], sem)
    copy.start()
    copy.wait()


def shards(mesh, visibilities, positions, tracks, counts, screens, offsets):
    n = mesh.shape["chan"]
    facets = mesh.shape["facet"]
    rows = visibilities.shape[-1]
    vmem = pl.BlockSpec(memory_space=pltpu.VMEM)
    anywhere = pl.BlockSpec(memory_space=pl.ANY)
    lines = n // 8 * 8 + 8
    facet_ring = [(i, (i + 1) % facets) for i in range(facets)]

    numbers = pl.pallas_call(
        functools.partial(numbers_kernel, n),
        out_shape=jax.ShapeDtypeStruct((lines, rows), jnp.float32),
        in_specs=[pl.BlockSpec(memory_space=pltpu.SMEM)] * 3,
        out_specs=vmem,
        compiler_params=pltpu.CompilerParams(vmem_limit_bytes=56 << 20),
    )(tracks, counts, offsets)
    pieces = exchange(n, lax.axis_index("chan"), visibilities, positions, numbers)
    screens_before = lax.ppermute(screens, "facet", facet_ring)
    ahead, behind, numbers = pl.pallas_call(
        tables_kernel,
        out_shape=(
            jax.ShapeDtypeStruct((2 * SUB, SUB), jnp.bfloat16),
            jax.ShapeDtypeStruct((2 * SUB, SUB), jnp.bfloat16),
            jax.ShapeDtypeStruct((lines, rows), jnp.float32),
        ),
        in_specs=[vmem],
        out_specs=(vmem, vmem, vmem),
        compiler_params=pltpu.CompilerParams(vmem_limit_bytes=8 << 20),
        cost_estimate=pl.CostEstimate(flops=4 << 20, bytes_accessed=1 << 20, transcendentals=0),
    )(numbers)
    payload = jnp.concatenate(pieces + [numbers], axis=0)

    depth = n * rows
    picture = jax.ShapeDtypeStruct((SUB, SUB), jnp.float32)
    scale = 1.0 / (2.0 * math.sqrt(n * rows))
    factor_rows = 2 * (4 * HALF + TILE + 2 * SUB)
    room = 24 + (2 * factor_rows * depth >> 20)

    def pictures_of(turn, *operands):
        spilled = turn == 2
        return pl.pallas_call(
            functools.partial(picture_kernel, n, scale, turn),
            out_shape=(jax.ShapeDtypeStruct((2, SUB, SUB), jnp.float32), picture),
            in_specs=[vmem, vmem if spilled else anywhere, vmem, vmem]
            + [vmem] * (len(operands) - 4),
            out_specs=(vmem, vmem),
            scratch_shapes=[
                pltpu.SMEM((1, rows), jnp.float32),
                pltpu.VMEM((4 * HALF + 2 * TILE, depth), jnp.bfloat16),
                pltpu.VMEM((4 * HALF, depth), jnp.bfloat16),
                pltpu.VMEM((2 * SUB, depth), jnp.bfloat16),
                pltpu.VMEM((2 * SUB, depth), jnp.bfloat16),
                pltpu.SemaphoreType.DMA((1 + PARTS,)),
            ]
            + [pltpu.VMEM((2, SUB, SUB), jnp.float32)] * (not spilled),
            compiler_params=pltpu.CompilerParams(
                vmem_limit_bytes=max(room << 20, 0 if spilled else 209 << 18)
            ),
            cost_estimate=pl.CostEstimate(
                flops=2 * depth * SUB * SUB * 4, bytes_accessed=4 << 20, transcendentals=0
            ),
        )(*operands)

    own, across = pictures_of(0, payload, screens, ahead, behind)
    payload, across = lax.optimization_barrier((payload, across))
    payload_before = lax.ppermute(payload, "facet", facet_ring)
    own_later, across_later = pictures_of(1, payload, screens, ahead, behind)
    before, across = pictures_of(
        2, payload_before, screens_before, ahead, behind, across, across_later
    )
    across = lax.ppermute(across, "chan", [(i, (i + 1) % n) for i in range(n)])
    image, block = pl.pallas_call(
        functools.partial(paste_kernel, n),
        out_shape=(jax.ShapeDtypeStruct((STRIP, BAND), jnp.float32), picture),
        in_specs=[anywhere] * 2 + [vmem] * 3,
        out_specs=(vmem, vmem),
        scratch_shapes=[pltpu.SMEM((2, rows), jnp.float32), pltpu.SemaphoreType.DMA((2,))],
        compiler_params=pltpu.CompilerParams(vmem_limit_bytes=16 << 20),
        cost_estimate=pl.CostEstimate(flops=1 << 20, bytes_accessed=12 << 20, transcendentals=0),
    )(payload, payload_before, own, own_later, before)
    return pl.pallas_call(
        finish_kernel,
        out_shape=jax.ShapeDtypeStruct((STRIP, BAND), jnp.float32),
        in_specs=[anywhere, vmem, vmem],
        out_specs=anywhere,
        scratch_shapes=[pltpu.VMEM((STRIP, SUB), jnp.float32), pltpu.SemaphoreType.DMA],
        input_output_aliases={0: 0},
        compiler_params=pltpu.CompilerParams(vmem_limit_bytes=4 << 20),
    )(image, block, across)


def solution(mesh):
    return jax.shard_map(
        functools.partial(shards, mesh),
        mesh=mesh,
        in_specs=(
            P("facet", "chan", None, None, None),
            P("facet", "chan", None, None, None),
            P("facet", "chan", None, None),
            P("facet", "chan", None),
            P("facet", "chan", None, None, None),
            P("facet", "chan", None, None),
        ),
        out_specs=P("facet", "chan"),
        check_vma=False,
    )
```

```python
import functools
import math

import jax
import jax.numpy as jnp
from jax import lax
from jax.experimental import pallas as pl
from jax.experimental.pallas import tpu as pltpu
from jax.sharding import PartitionSpec as P

TAPS = 8
STRIP = 256
BAND = 4096
SUB = 256
HALF = SUB // 2
BLOCK = 64
TILE = 16
LAST = BAND // SUB - 1
PARTS = 2


def numbers_kernel(n, tracks, counts, offsets, out):
    me = lax.axis_index("chan")
    lane = lax.broadcasted_iota(jnp.int32, (1, out.shape[1]), 1)
    block = lane // BLOCK
    lines = []
    for k in range(n):
        source = sender(n, me, k)
        target = jnp.zeros_like(lane)
        for b in range(tracks.shape[-1]):
            target = jnp.where(block == b, tracks[0, 0, source, b], target)
        lines.append(jnp.where(block < counts[0, 0, source], target + 1, 0))
    corners = jnp.zeros_like(lane)
    for place in range(4):
        corners = jnp.where(lane == place, offsets[0, 0, place // 2, place % 2], corners)
    lines = [corners] + lines + [corners] * (out.shape[0] - n - 1)
    out[...] = jnp.concatenate(lines, axis=0).astype(jnp.float32)


def tables_kernel(numbers_in, ahead, behind, numbers):
    numbers[...] = numbers_in[...]
    shape = (SUB, SUB)
    for across, out in ((1, ahead), (0, behind)):
        j = lax.broadcasted_iota(jnp.int32, shape, across)
        x = lax.broadcasted_iota(jnp.int32, shape, 1 - across)
        turn = jnp.where(j > HALF, (j - HALF) * x + 3 * SUB // 4, j * x) & (SUB - 1)
        turn = jnp.minimum(turn, SUB - turn).astype(jnp.float32)
        half_angle = cosine(turn * (math.pi / SUB))
        high, low = halves(2.0 * half_angle * half_angle - 1.0)
        out[:SUB] = high
        out[SUB:] = low


def halves(value):
    high = value.astype(jnp.bfloat16)
    low = (value - high.astype(jnp.float32)).astype(jnp.bfloat16)
    return high, low


def cosine(angle):
    square = angle * angle
    series = jnp.float32(-1.0 / math.factorial(14))
    for order in range(12, -1, -2):
        sign = 1.0 if order % 4 == 0 else -1.0
        series = series * square + jnp.float32(sign / math.factorial(order))
    return series


def taper(offset):
    series = cosine(offset * (math.pi / TAPS))
    return jnp.where(jnp.abs(offset) < TAPS / 2, series * series, 0.0)


def folded(position, rho):
    base = jnp.floor(position) - (TAPS // 2 - 1)

    def cell_at(residue):
        ahead = residue - base
        ahead = ahead - TILE * jnp.floor(ahead * (1.0 / TILE))
        return base + ahead, ahead < TAPS

    cell, inside = cell_at(rho)
    direct = inside & (cell <= HALF)
    near = jnp.where(direct, taper(cell - position), 0.0)
    mirror, inside = cell_at(-rho)
    far = jnp.where(inside & (mirror > HALF), taper(mirror - position), 0.0)
    turn = jnp.where(direct, cell - rho, SUB - mirror - rho) * (1.0 / TILE)
    return near + far, near - far, turn.astype(jnp.bfloat16)


def sender(n, me, k):
    return me ^ k if n == 4 else lax.rem(me - k + n, n)


def exchange(n, me, visibilities, positions, numbers):
    def slot(index):
        parts = [lax.dynamic_index_in_dim(a[0, 0], index, 0, False) for a in (visibilities, positions)]
        return jnp.concatenate(parts, axis=0)

    def swap(piece, bit):
        return lax.ppermute(piece, "chan", [(i, i ^ bit) for i in range(n)])

    if n != 4:
        pieces = [slot(me)]
        for k in range(1, n):
            ring = [(i, (i + k) % n) for i in range(n)]
            pieces.append(lax.ppermute(slot(lax.rem(me + k, n)), "chan", ring))
        return pieces
    near = swap(jnp.concatenate([slot(me ^ 1), slot(me ^ 3)], axis=0), 1)
    near, numbers = lax.optimization_barrier((near, numbers))
    far = swap(jnp.concatenate([slot(me ^ 2), near[4:]], axis=0), 2)
    return [slot(me), near[:4], far]


def fill_factors(n, payload, le, lo, we, wo):
    rows = payload.shape[-1]
    rho = lax.broadcasted_iota(jnp.int32, (TILE, rows), 0).astype(jnp.float32)
    zero = jnp.zeros((TILE, rows), jnp.bfloat16)
    for k in range(n):
        piece = payload[4 * k : 4 * k + 4]
        target = payload[4 * n + 1 + k : 4 * n + 2 + k]
        real = jnp.where(target > 0.0, piece[0:1], 0.0)
        imag = jnp.where(target > 0.0, piece[1:2], 0.0)
        u_position = piece[2:3]
        u_even, u_odd, u_turn = folded(u_position, rho)
        v_even, v_odd, v_turn = folded(piece[3:4], rho)
        middle = taper(HALF - u_position)
        place = pl.ds(k * rows, rows)

        def put(ref, row, pair):
            for part, value in enumerate(pair):
                start = part * (ref.shape[0] // 2) + row
                ref[start : start + TILE, place] = value

        first = target < 2.0
        evens = [halves(jnp.where(first, u_even, 0.0)), halves(jnp.where(first, 0.0, u_even))]
        odds = [halves(jnp.where(first, u_odd, 0.0)), halves(jnp.where(first, 0.0, u_odd))]
        for turn in range(HALF // TILE):
            chosen = u_turn == turn
            for s in range(2):
                row = s * HALF + turn * TILE
                put(le, row, [jnp.where(chosen, e, zero) for e in evens[s]])
                put(lo, row, [jnp.where(chosen, o, zero) for o in odds[s]])
        middles = jnp.where(
            (rho == 0) & first, middle, jnp.where((rho == 8) & jnp.logical_not(first), middle, 0.0)
        )
        put(le, 2 * HALF, halves(middles))
        for ref, cosine, sine in (
            (we, real * v_even, imag * v_odd),
            (wo, imag * v_even, -real * v_odd),
        ):
            cosine, sine = halves(cosine), halves(sine)
            for turn in range(HALF // TILE):
                chosen = v_turn == turn
                put(ref, turn * TILE, [jnp.where(chosen, c, zero) for c in cosine])
                pair = [jnp.where(chosen, c, zero) for c in sine]
                if turn == 0:
                    top = v_turn == HALF // TILE
                    pair = [jnp.where(top, c, p) for c, p in zip(cosine, pair)]
                put(ref, HALF + turn * TILE, pair)


def product(a, b, contract):
    rows, half = a.shape[0] // 2, b.shape[0] // 2

    def dot(left, right):
        numbers = (((1,), (contract,)), ((), ()))
        return lax.dot_general(left, right, numbers, preferred_element_type=jnp.float32)

    main = dot(a, b[:half])
    return main[:rows] + main[rows:] + dot(a[:rows], b[half:])


def picture_kernel(n, scale, turn, *refs):
    if turn < 2:

        @pl.when(lax.rem(lax.axis_index("facet"), 2) == 1 - turn)
        def _():
            make_pictures(n, scale, False, *refs)

    else:
        make_pictures(n, scale, True, *refs)


def own_part(first, second):
    return jnp.where(lax.rem(lax.axis_index("facet"), 2) == 1, first, second)


def make_pictures(n, scale, spilled, *refs):
    count = 6 if spilled else 4
    payload, screens_in, ahead, behind = refs[:4]
    pictures, across = refs[count : count + 2]
    corners, le, lo, we, wo, sems = refs[count + 2 : count + 8]
    copies = [pltpu.make_async_copy(payload.at[pl.ds(4 * n, 1)], corners, sems.at[0])]
    if spilled:
        screens = screens_in.at[0, 0]
    else:
        screens = refs[-1]
        for part in range(PARTS):
            place = (part * 2 // PARTS, pl.ds(part % (PARTS // 2) * (2 * SUB // PARTS), 2 * SUB // PARTS))
            copies.append(
                pltpu.make_async_copy(
                    screens_in.at[0, 0].at[place], screens.at[place], sems.at[1 + part]
                )
            )
    for copy in copies:
        copy.start()
    fill_factors(n, payload, le, lo, we, wo)
    even = product(le[...], we[...], 1)
    odd = product(lo[...], wo[...], 1)
    row_ids = lax.broadcasted_iota(jnp.int32, (SUB, SUB), 0)
    col_ids = lax.broadcasted_iota(jnp.int32, (SUB, SUB), 1)
    first_row = lax.broadcasted_iota(jnp.int32, (HALF, SUB), 0) == 0
    total = own_part(refs[4][...], refs[5][...]) if spilled else jnp.zeros((SUB, SUB), jnp.float32)
    grids = []
    for s in range(2):
        middle = even[2 * HALF + 8 * s : 2 * HALF + 8 * s + 1]
        lower = jnp.where(first_row, middle, odd[s * HALF : (s + 1) * HALF])
        grids += [even[s * HALF : (s + 1) * HALF], lower]
    half_way = product(
        jnp.concatenate(halves(jnp.concatenate(grids, axis=0)), axis=0), behind[...], 0
    )
    for s in range(2):
        image = jnp.concatenate(halves(half_way[s * SUB : (s + 1) * SUB]), axis=0)
        image = product(ahead[...], image, 0)
        if s == 0:
            copies[0].wait()
        for copy in copies[1 + s * PARTS // 2 : 1 + (s + 1) * PARTS // 2]:
            copy.wait()
        image = screens[s] * (image * scale)
        row = corners[0, 2 * s].astype(jnp.int32)
        col = corners[0, 2 * s + 1].astype(jnp.int32)
        shift = lax.rem(col, SUB)
        image = pltpu.roll(pltpu.roll(image, row, 0), shift, 1)
        here = (row_ids < row) if spilled else (row_ids >= row)
        image = jnp.where(here, image, 0.0)
        pictures[s] = image
        beyond = (col_ids < shift) & (col // SUB == LAST)
        total = total + jnp.where(beyond, image, 0.0)
    across[...] = total


def paste_kernel(n, payload_in, payload_before, own, own_later, before, out, block_out, corners, sems):
    copies = [
        pltpu.make_async_copy(source.at[pl.ds(4 * n, 1)], corners.at[pl.ds(i, 1)], sems.at[i])
        for i, source in enumerate((payload_in, payload_before))
    ]
    for copy in copies:
        copy.start()
    out[...] = jnp.zeros_like(out)
    for copy in copies:
        copy.wait()
    col_ids = lax.broadcasted_iota(jnp.int32, (SUB, SUB), 1)
    for i, pictures in enumerate((own, before)):
        for s in range(2):
            col = corners[i, 2 * s + 1].astype(jnp.int32)
            shift = lax.rem(col, SUB)
            block = col // SUB
            image = pictures[s] if i else own_part(own[s], own_later[s])
            place = pl.ds(pl.multiple_of(block * SUB, SUB), SUB)
            out[:, place] += jnp.where(col_ids >= shift, image, 0.0)

            @pl.when(block < LAST)
            def _():
                place = pl.ds(pl.multiple_of((block + 1) * SUB, SUB), SUB)
                out[:, place] += jnp.where(col_ids < shift, image, 0.0)

    block_out[...] = out[:, :SUB]


def finish_kernel(image_in, block, across, image_out, total, sem):
    total[...] = block[...] + across[...]
    copy = pltpu.make_async_copy(total, image_out.at[:, pl.ds(0, SUB)], sem)
    copy.start()
    copy.wait()


def shards(mesh, visibilities, positions, tracks, counts, screens, offsets):
    n = mesh.shape["chan"]
    facets = mesh.shape["facet"]
    rows = visibilities.shape[-1]
    vmem = pl.BlockSpec(memory_space=pltpu.VMEM)
    anywhere = pl.BlockSpec(memory_space=pl.ANY)
    lines = n // 8 * 8 + 8
    facet_ring = [(i, (i + 1) % facets) for i in range(facets)]

    numbers = pl.pallas_call(
        functools.partial(numbers_kernel, n),
        out_shape=jax.ShapeDtypeStruct((lines, rows), jnp.float32),
        in_specs=[pl.BlockSpec(memory_space=pltpu.SMEM)] * 3,
        out_specs=vmem,
        compiler_params=pltpu.CompilerParams(vmem_limit_bytes=56 << 20),
    )(tracks, counts, offsets)
    pieces = exchange(n, lax.axis_index("chan"), visibilities, positions, numbers)
    screens_before = lax.ppermute(screens, "facet", facet_ring)
    ahead, behind, numbers = pl.pallas_call(
        tables_kernel,
        out_shape=(
            jax.ShapeDtypeStruct((2 * SUB, SUB), jnp.bfloat16),
            jax.ShapeDtypeStruct((2 * SUB, SUB), jnp.bfloat16),
            jax.ShapeDtypeStruct((lines, rows), jnp.float32),
        ),
        in_specs=[vmem],
        out_specs=(vmem, vmem, vmem),
        compiler_params=pltpu.CompilerParams(vmem_limit_bytes=8 << 20),
        cost_estimate=pl.CostEstimate(flops=4 << 20, bytes_accessed=1 << 20, transcendentals=0),
    )(numbers)
    payload = jnp.concatenate(pieces + [numbers], axis=0)

    depth = n * rows
    picture = jax.ShapeDtypeStruct((SUB, SUB), jnp.float32)
    scale = 1.0 / (2.0 * math.sqrt(n * rows))
    factor_rows = 2 * (4 * HALF + TILE + 2 * SUB)
    room = 24 + (2 * factor_rows * depth >> 20)

    def pictures_of(turn, *operands):
        spilled = turn == 2
        return pl.pallas_call(
            functools.partial(picture_kernel, n, scale, turn),
            out_shape=(jax.ShapeDtypeStruct((2, SUB, SUB), jnp.float32), picture),
            in_specs=[vmem, vmem if spilled else anywhere, vmem, vmem]
            + [vmem] * (len(operands) - 4),
            out_specs=(vmem, vmem),
            scratch_shapes=[
                pltpu.SMEM((1, rows), jnp.float32),
                pltpu.VMEM((4 * HALF + 2 * TILE, depth), jnp.bfloat16),
                pltpu.VMEM((4 * HALF, depth), jnp.bfloat16),
                pltpu.VMEM((2 * SUB, depth), jnp.bfloat16),
                pltpu.VMEM((2 * SUB, depth), jnp.bfloat16),
                pltpu.SemaphoreType.DMA((1 + PARTS,)),
            ]
            + [pltpu.VMEM((2, SUB, SUB), jnp.float32)] * (not spilled),
            compiler_params=pltpu.CompilerParams(
                vmem_limit_bytes=max(room << 20, 0 if spilled else 209 << 18)
            ),
            cost_estimate=pl.CostEstimate(
                flops=2 * depth * SUB * SUB * 4, bytes_accessed=4 << 20, transcendentals=0
            ),
        )(*operands)

    own, across = pictures_of(0, payload, screens, ahead, behind)
    payload, across = lax.optimization_barrier((payload, across))
    payload_before = lax.ppermute(payload, "facet", facet_ring)
    own_later, across_later = pictures_of(1, payload, screens, ahead, behind)
    before, across = pictures_of(
        2, payload_before, screens_before, ahead, behind, across, across_later
    )
    across = lax.ppermute(across, "chan", [(i, (i + 1) % n) for i in range(n)])
    image, block = pl.pallas_call(
        functools.partial(paste_kernel, n),
        out_shape=(jax.ShapeDtypeStruct((STRIP, BAND), jnp.float32), picture),
        in_specs=[anywhere] * 2 + [vmem] * 3,
        out_specs=(vmem, vmem),
        scratch_shapes=[pltpu.SMEM((2, rows), jnp.float32), pltpu.SemaphoreType.DMA((2,))],
        compiler_params=pltpu.CompilerParams(vmem_limit_bytes=16 << 20),
        cost_estimate=pl.CostEstimate(flops=1 << 20, bytes_accessed=12 << 20, transcendentals=0),
    )(payload, payload_before, own, own_later, before)
    return pl.pallas_call(
        finish_kernel,
        out_shape=jax.ShapeDtypeStruct((STRIP, BAND), jnp.float32),
        in_specs=[anywhere, vmem, vmem],
        out_specs=anywhere,
        scratch_shapes=[pltpu.VMEM((STRIP, SUB), jnp.float32), pltpu.SemaphoreType.DMA],
        input_output_aliases={0: 0},
        compiler_params=pltpu.CompilerParams(vmem_limit_bytes=4 << 20),
    )(image, block, across)


def solution(mesh):
    return jax.shard_map(
        functools.partial(shards, mesh),
        mesh=mesh,
        in_specs=(
            P("facet", "chan", None, None, None),
            P("facet", "chan", None, None, None),
            P("facet", "chan", None, None),
            P("facet", "chan", None),
            P("facet", "chan", None, None, None),
            P("facet", "chan", None, None),
        ),
        out_specs=P("facet", "chan"),
        check_vma=False,
    )
```
